256 devices in a mesh: ctx: 32 (over z, x_hi, core), head: 8 (over x_lo, y).
Axes of the slice: x: 4 (x_hi: 2, x_lo: 2; x = x_hi * 2 + x_lo), y: 4, z: 8, core: 2. Of those that a mesh axis runs over, the one named last changes fastest.
Arguments:
- tokens: bfloat16 [8192, 4096], P('ctx', 'head'), may hold values from -26 to 26
- w_query: bfloat16 [4096, 2048], P('ctx', 'head'), may hold values from -0.09375 to 0.09375, as said below
- w_key: bfloat16 [4096, 2048], P('ctx', 'head'), may hold values from -1.5 to 1.5
- w_value: bfloat16 [4096, 2048], P('ctx', 'head'), may hold values from -0.09375 to 0.09375
- w_out: bfloat16 [2048, 4096], P('head', 'ctx'), may hold values from -0.125 to 0.125
- query_down: bfloat16 [4096, 8], replicated, may hold values from -0.09375 to 0.09375
- query_up: bfloat16 [8, 2048], P(None, 'head'), may hold values from -0.5 to 0.5
- value_down: bfloat16 [4096, 8], replicated, may hold values from -0.09375 to 0.09375
- value_up: bfloat16 [8, 2048], P(None, 'head'), may hold values from -0.5 to 0.5
- shifted: int32 [16], replicated, may hold values from 0 to 1, as said below
- grad_out: bfloat16 [8192, 4096], P('ctx', 'head'), may hold values from -6 to 6
Outputs:
- output: bfloat16 [8192, 4096], P('ctx', 'head')
- grad_tokens: bfloat16 [8192, 4096], P('ctx', 'head')
- grad_query_down: float32 [4096, 8], replicated
- grad_query_up: float32 [8, 2048], P(None, 'head')
- grad_value_down: float32 [4096, 8], replicated
- grad_value_up: float32 [8, 2048], P(None, 'head')
The draws below stay inside these ranges and needn't reach their ends.
Inputs may be any that keep to these rules, and one draw needn't show every extreme that they name: Exactly 8 of the heads are shifted. `w_query`: entries within 6 / sqrt(4096).
All inputs are finite; a program needn't handle non-finite values.
Results may differ from the reference program's by a relative error of at most 0.0095.
The reference program's roundings to bfloat16 on the way (of `normed`, `low_q`, `query`, `prob`, `context`, `d_context`, `dscore` and `dq_pre`) count: a program that leaves them out, or rounds other values in their place, can miss the bound.
Values may be sent and summed in bfloat16 or wider, within the bound.
No kernel may reach another device: no remote copies, remote signals or barrier semaphores. Data moves between devices by JAX's collectives and lax.ppermute only.
A program may use at most 128 MiB of HBM per device.

```python
import math
import jax
import jax.numpy as jnp
from jax import lax

D = 4096
HEADS = 16
HEAD_DIM = 128
RANK = 8
HD = 2048
SEQ = 8192
GROUP = 2048
SHIFT = 1024


def shared_base(key):
    return jnp.clip(jax.random.normal(key, (D, HD), jnp.float32), -6.0, 6.0)


def draw_w_query(key, part):
    base = shared_base(key)
    return (base * D ** (-0.5)).astype(jnp.bfloat16)


def draw_w_key(key, part):
    key = jax.random.fold_in(key, 12)
    first = jax.random.fold_in(key, 0)
    result = jnp.clip(jax.random.normal(first, (D, HD), jnp.float32), -6.0, 6.0) * D ** (-0.5)
    return result.astype(jnp.bfloat16)


def draw_tokens(key, part):
    key = jax.random.fold_in(key, 14)
    first, second = jax.random.split(key)
    ramp = jnp.arange(D, dtype=jnp.float32) / (D - 1)
    rough = jnp.exp(jax.random.uniform(second, (D,), jnp.float32, math.log(0.7), math.log(1.4)))
    column = 0.3 * jnp.exp(ramp * math.log(10.0)) * rough
    values = jnp.clip(jax.random.normal(first, (SEQ, D), jnp.float32), -6.0, 6.0)
    return (values * column[None, :]).astype(jnp.bfloat16)


def draw_shifted(key, part):
    key = jax.random.fold_in(key, 13)
    order = jax.random.permutation(key, HEADS)
    return (order < HEADS // 2).astype(jnp.int32)


def shard_levels(rng, dims, shards, smallest, top_value):
    loudness = 1.0
    for position, shards_of in shards:
        steps = jax.random.uniform(jax.random.fold_in(jax.random.fold_in(rng, 6), position), (shards_of,), jnp.float32, smallest / len(shards), top_value / len(shards))
        loudness = loudness * jnp.repeat(jnp.exp(steps), dims[position] // shards_of).reshape((-1,) + (1,) * (len(dims) - 1 - position))
    return loudness


def centred(rng, dims, deviation, limit, cuts=(), held_as=jnp.bfloat16):
    values = jax.random.normal(rng, dims, jnp.float32) * deviation
    if len(cuts) > 0:
        values = shard_levels(rng, dims, cuts, -0.22, 0.18) * values
    return jnp.clip(values, min=-limit, max=limit).astype(held_as)


def setup_inputs(seed: int = 0) -> dict:
    seeds = jax.random.split(jax.random.key(seed), 12)
    tokens = draw_tokens(jax.random.fold_in(seeds[11], 71), 0)
    w_query = draw_w_query(jax.random.fold_in(seeds[11], 71), 0)
    w_key = draw_w_key(jax.random.fold_in(seeds[11], 71), 0)
    w_value = centred(seeds[3], (D, HD), D ** -0.5, 0.09375, ((0, 32), (1, 8)))
    w_out = centred(seeds[4], (HD, D), HD ** -0.5, 0.125, ((0, 8), (1, 32)))
    query_down = centred(seeds[5], (D, RANK), D ** -0.5, 0.09375)
    query_up = centred(seeds[6], (RANK, HD), (RANK * 16) ** -0.5, 0.5, ((1, 8),))
    value_down = centred(seeds[7], (D, RANK), D ** -0.5, 0.09375)
    value_up = centred(seeds[8], (RANK, HD), (RANK * 16) ** -0.5, 0.5, ((1, 8),))
    shifted = draw_shifted(jax.random.fold_in(seeds[11], 71), 0)
    grad_out = centred(seeds[10], (SEQ, D), 1.0, 6.0, ((0, 32), (1, 8)))
    return dict(tokens=tokens, w_query=w_query, w_key=w_key, w_value=w_value, w_out=w_out, query_down=query_down, query_up=query_up, value_down=value_down, value_up=value_up, shifted=shifted, grad_out=grad_out)


def rope(values, positions, sign):
    count = values.shape[0]
    shaped = values.reshape(count, values.shape[1] // HEAD_DIM, HEAD_DIM)
    half = HEAD_DIM // 2
    freq = jnp.power(10000.0, -jnp.arange(half, dtype=jnp.float32) * 2.0 / HEAD_DIM)
    angle = positions.astype(jnp.float32)[:, None] * freq[None, :]
    cosine = jnp.cos(angle)[:, None, :]
    sine = sign * jnp.sin(angle)[:, None, :]
    first = shaped[:, :, :half]
    second = shaped[:, :, half:]
    rotated = jnp.concatenate([first * cosine - second * sine, second * cosine + first * sine], axis=2)
    return rotated.reshape(count, values.shape[1])

def head_pass(packed):
    query, key, value, d_context, offset = packed
    groups = SEQ // GROUP
    scale = 1.0 / HEAD_DIM ** 0.5

    def rolled(array):
        return jnp.roll(array, -offset, axis=0).reshape(groups, GROUP, HEAD_DIM).astype(jnp.float32)
    query_r = rolled(query)
    key_r = rolled(key)
    value_r = rolled(value)
    dctx_r = rolled(d_context)
    scores = jnp.einsum('gqd,gkd->gqk', query_r, key_r) * scale
    allowed = jnp.tril(jnp.ones((GROUP, GROUP), dtype=bool))[None]
    scores = jnp.where(allowed, scores, -jnp.inf)
    top = lax.optimization_barrier(jnp.max(scores, axis=-1, keepdims=True))
    expo = jnp.exp(scores - top)
    prob32 = expo / lax.optimization_barrier(jnp.sum(expo, axis=-1, keepdims=True))
    prob = prob32.astype(jnp.bfloat16)
    context = jnp.einsum('gqk,gkd->gqd', prob.astype(jnp.float32), value_r).astype(jnp.bfloat16)
    dprob = jnp.einsum('gqd,gkd->gqk', dctx_r, value_r)
    delta = lax.optimization_barrier(jnp.sum(prob32 * dprob, axis=-1, keepdims=True))
    dscore = (prob32 * (dprob - delta) * scale).astype(jnp.bfloat16).astype(jnp.float32)
    grad_q = jnp.einsum('gqk,gkd->gqd', dscore, key_r)
    grad_k = jnp.einsum('gqk,gqd->gkd', dscore, query_r)
    grad_v = jnp.einsum('gqk,gqd->gkd', prob.astype(jnp.float32), dctx_r)

    def back(array):
        return jnp.roll(array.reshape(SEQ, HEAD_DIM), offset, axis=0)
    return (back(context), back(grad_q), back(grad_k), back(grad_v))

def reference(tokens, w_query, w_key, w_value, w_out, query_down, query_up, value_down, value_up, shifted, grad_out):
    tokens32 = tokens.astype(jnp.float32)
    rinv = lax.rsqrt(lax.optimization_barrier(jnp.mean(tokens32 * tokens32, axis=-1, keepdims=True)) + 1e-05)
    xn = tokens32 * rinv
    normed = xn.astype(jnp.bfloat16)
    low_q = jnp.dot(normed, query_down, preferred_element_type=jnp.float32).astype(jnp.bfloat16)
    low_v = jnp.dot(normed, value_down, preferred_element_type=jnp.float32).astype(jnp.bfloat16)
    positions = jnp.arange(SEQ, dtype=jnp.int32)
    q_lin = jnp.dot(normed, w_query, preferred_element_type=jnp.float32) + 2.0 * jnp.dot(low_q, query_up, preferred_element_type=jnp.float32)
    query = rope(q_lin, positions, 1.0).astype(jnp.bfloat16)
    key = rope(jnp.dot(normed, w_key, preferred_element_type=jnp.float32), positions, 1.0).astype(jnp.bfloat16)
    value = (jnp.dot(normed, w_value, preferred_element_type=jnp.float32) + 2.0 * jnp.dot(low_v, value_up, preferred_element_type=jnp.float32)).astype(jnp.bfloat16)
    d_context = jnp.dot(grad_out, w_out.T, preferred_element_type=jnp.float32).astype(jnp.bfloat16)

    def split(array):
        return array.reshape(SEQ, HEADS, HEAD_DIM).transpose(1, 0, 2)

    def merge(array):
        return array.transpose(1, 0, 2).reshape(SEQ, HD)
    offsets = (shifted * SHIFT).astype(jnp.int32)
    context, grad_q, grad_k, grad_v = lax.map(head_pass, (split(query), split(key), split(value), split(d_context), offsets))
    attn = jnp.dot(merge(context), w_out, preferred_element_type=jnp.float32)
    output = (tokens32 + attn).astype(jnp.bfloat16)
    dq_pre = rope(merge(grad_q), positions, -1.0).astype(jnp.bfloat16)
    dk_pre = rope(merge(grad_k), positions, -1.0).astype(jnp.bfloat16)
    dv_b = merge(grad_v).astype(jnp.bfloat16)
    g_q = jnp.dot(dq_pre, query_up.T, preferred_element_type=jnp.float32)
    g_v = jnp.dot(dv_b, value_up.T, preferred_element_type=jnp.float32)
    d_normed = jnp.dot(dq_pre, w_query.T, preferred_element_type=jnp.float32)
    d_normed = d_normed + jnp.dot(dk_pre, w_key.T, preferred_element_type=jnp.float32)
    d_normed = d_normed + jnp.dot(dv_b, w_value.T, preferred_element_type=jnp.float32)
    d_normed = d_normed + 2.0 * jnp.dot(g_q, query_down.astype(jnp.float32).T, precision=lax.Precision.HIGHEST)
    d_normed = d_normed + 2.0 * jnp.dot(g_v, value_down.astype(jnp.float32).T, precision=lax.Precision.HIGHEST)
    row_mean = lax.optimization_barrier(jnp.sum(d_normed * xn, axis=-1, keepdims=True)) / D
    grad_tokens = (grad_out.astype(jnp.float32) + rinv * (d_normed - xn * row_mean)).astype(jnp.bfloat16)
    scale_out = 1.0 / SEQ ** 0.5
    normed32 = normed.astype(jnp.float32)
    grad_query_down = 2.0 * jnp.dot(normed32.T, g_q, precision=lax.Precision.HIGHEST) * scale_out
    grad_value_down = 2.0 * jnp.dot(normed32.T, g_v, precision=lax.Precision.HIGHEST) * scale_out
    grad_query_up = 2.0 * jnp.dot(low_q.T, dq_pre, preferred_element_type=jnp.float32) * scale_out
    grad_value_up = 2.0 * jnp.dot(low_v.T, dv_b, preferred_element_type=jnp.float32) * scale_out
    return (output, grad_tokens, grad_query_down, grad_query_up, grad_value_down, grad_value_up)
```

```python
import functools

import jax
import jax.numpy as jnp
from jax import lax
from jax.experimental import pallas as pl
from jax.experimental.pallas import tpu as pltpu
from jax.sharding import PartitionSpec as P

HEAD_DIM = 128
BF = jnp.bfloat16
F32 = jnp.float32
CTX = 32
HEAD = 8
Z = 8
ROWS = 256
SCALE = 1.0 / HEAD_DIM**0.5
HIDDEN = -1e30
DELTA = (0, -1, 1, -2, 2, -3, 3, 4)
VMEM_LIMIT = 40 * 1024 * 1024


def move(value, axis, count, to):
    return lax.ppermute(value, axis, [(i, to(i)) for i in range(count)])


def swap_core(value):
    return move(value, "ctx", CTX, lambda i: i ^ 1)


def swap_x(value):
    return move(value, "ctx", CTX, lambda i: i ^ 2)


def along_z(value, step):
    return move(value, "ctx", CTX, lambda i: (i + 4 * step) % CTX)


def chips(value, step, back=False):
    pairs = [(i, (i + 2 * step) % CTX) for i in range(CTX)]
    if step == 3:
        pairs = [p for p in pairs if (p[1] // 2) % 2 == 1]
    if back:
        pairs = [(d, s) for s, d in pairs]
    return lax.ppermute(value, "ctx", pairs)


def core_first(value):
    lead = value.shape[:-1]
    return value.reshape(*lead, 2, 2, 128).swapaxes(-3, -2).reshape(*lead, 512)


def ring(pack, x_place):
    other = swap_x(pack)
    block = jnp.where(
        x_place == 0,
        jnp.concatenate([pack, other], 1),
        jnp.concatenate([other, pack], 1),
    )
    up = down = block
    parts = [block]
    for _ in range(3):
        up = along_z(up, 1)
        down = along_z(down, -1)
        parts += [up, down]
    half = block.shape[1] // 2
    parts += [along_z(up[:, :half], 1), along_z(down[:, half:], -1)]
    return parts, [swap_core(p) for p in parts]


def share(value):
    sent = jnp.broadcast_to(value[None], (HEAD,) + value.shape)
    return lax.all_to_all(sent, "head", 0, 0)


def nn(a, b):
    return jnp.dot(a, b, preferred_element_type=F32)


def nt(a, b):
    return lax.dot_general(a, b, (((1,), (1,)), ((), ())), preferred_element_type=F32)


def tn(a, b):
    return lax.dot_general(a, b, (((0,), (0,)), ((), ())), preferred_element_type=F32)


def whole(shape_dtypes, n_in, kernel, args, scratch=(), flops=0):
    specs = [pl.BlockSpec(memory_space=pltpu.SMEM)]
    specs += [pl.BlockSpec(memory_space=pltpu.VMEM)] * n_in
    moved = sum(a.size * a.dtype.itemsize for a in args)
    return pl.pallas_call(
        kernel,
        out_shape=[jax.ShapeDtypeStruct(s, d) for s, d in shape_dtypes],
        in_specs=specs,
        out_specs=[pl.BlockSpec(memory_space=pltpu.VMEM)] * len(shape_dtypes),
        scratch_shapes=list(scratch),
        compiler_params=pltpu.CompilerParams(vmem_limit_bytes=VMEM_LIMIT),
        cost_estimate=pl.CostEstimate(flops=flops, bytes_accessed=moved, transcendentals=0),
    )(*args)


def place_of(at):
    return at[0], at[1]


def chunk_at(z, step):
    return lax.rem(z + (DELTA[step] + Z), Z)


def columns(core):
    return pl.ds(pl.multiple_of(core * 256, 256), 256)


def weight(mine, step, j):
    if step < 7:
        return mine[step][j]
    return jnp.concatenate([mine[7][j], mine[8][j]], 0)


def turn(v, table):
    return v * table[0] + pltpu.roll(v, 64, 1) * table[1]


def project_kernel(at, x, down, ups, table, *refs):
    mine, theirs = refs[:9], refs[9:18]
    query, keyval, rinv_out, low_out, normed = refs[18:]
    z, core = place_of(at)
    total = jnp.zeros((ROWS, 1), F32)
    for i in range(Z):
        part = x[i].astype(F32)
        total = total + jnp.sum(part * part, axis=1, keepdims=True)
    rinv = lax.rsqrt(total / 4096.0 + 1e-05)
    rinv_out[...] = jnp.broadcast_to(rinv, (ROWS, 128))
    low = jnp.zeros((ROWS, 16), F32)
    for i in range(Z):
        rounded = (x[i].astype(F32) * rinv).astype(BF)
        normed[i] = rounded
        low = low + nt(rounded, down[i])
    low = low.astype(BF)
    low_out[...] = low
    acc = [jnp.zeros((ROWS, 256), F32) for _ in range(3)]
    for step in range(Z):
        here = chunk_at(z, step)
        for side, parity in ((mine, core), (theirs, 1 - core)):
            a = normed[here, :, columns(parity)]
            for j in range(3):
                acc[j] = acc[j] + nn(a, weight(side, step, j))
    extra = 2.0 * nn(low, ups[...])
    q_lin = acc[0] + extra[:, :256]
    for h in range(2):
        cols = slice(h * 128, h * 128 + 128)
        query[:, cols] = turn(q_lin[:, cols], table).astype(BF)
        keyval[0, :, cols] = turn(acc[1][:, cols], table).astype(BF)
    keyval[1] = (acc[2] + extra[:, 256:]).astype(BF)


def context_grad_kernel(at, dy, *refs):
    mine, theirs = refs[:9], refs[9:18]
    out = refs[18]
    z, core = place_of(at)
    acc = jnp.zeros((ROWS, 256), F32)
    for step in range(Z):
        here = chunk_at(z, step)
        for side, parity in ((mine, core), (theirs, 1 - core)):
            acc = acc + nn(dy[here, :, columns(parity)], weight(side, step, 0))
    out[...] = acc.astype(BF)


def score_block(at, q, key, b, head):
    core, spot = at[1], at[2 + head]
    s = nt(q, key) * SCALE
    if b == 0:
        row = lax.broadcasted_iota(jnp.int32, (ROWS, ROWS), 0)
        col = lax.broadcasted_iota(jnp.int32, (ROWS, ROWS), 1)
        return jnp.where(col <= row, s, HIDDEN)
    behind = 2 * b if b < 4 else 2 * (b - 4) + 2 * core - 1
    seen = jnp.logical_and(behind > 0, behind <= spot)
    return s + jnp.where(seen, 0.0, HIDDEN)


def forward_kernel(at, query, *refs):
    blocks, mine, theirs = refs[:8], refs[8:17], refs[17:26]
    out, stats, scores, context = refs[26:]
    z, core = place_of(at)
    for head in range(2):
        cols = slice(head * 128, head * 128 + 128)
        q = query[:, cols]
        top = jnp.full((ROWS, 1), HIDDEN, F32)
        for b in range(8):
            s = score_block(at, q, blocks[b][0, :, cols], b, head)
            scores[b] = s
            top = jnp.maximum(top, jnp.max(s, axis=1, keepdims=True))
        total = jnp.zeros((ROWS, 1), F32)
        for b in range(8):
            e = jnp.exp(scores[b] - top)
            scores[b] = e
            total = total + jnp.sum(e, axis=1, keepdims=True)
        inv = 1.0 / total
        acc = jnp.zeros((ROWS, 128), F32)
        for b in range(8):
            acc = acc + nn((scores[b] * inv).astype(BF), blocks[b][1, :, cols])
        context[:, cols] = acc.astype(BF)
        stats[2 * head] = jnp.broadcast_to(top, (ROWS, 128))
        stats[2 * head + 1] = jnp.broadcast_to(inv, (ROWS, 128))
    for step in range(Z):
        here = chunk_at(z, step)
        for side, parity in ((mine, core), (theirs, 1 - core)):
            out[here, :, columns(parity)] = nt(context[...], weight(side, step, 0)).astype(BF)


def backward_kernel(at, query, d_context, table, stats, *refs):
    blocks = refs[:8]
    dq_out, kept, sent, probs, dprobs = refs[8:]
    for head in range(2):
        cols = slice(head * 128, head * 128 + 128)
        q = query[:, cols]
        d_ctx = d_context[:, cols]
        top = stats[2 * head][:, :1]
        inv = stats[2 * head + 1][:, :1]
        delta = jnp.zeros((ROWS, 1), F32)
        for b in range(8):
            s = score_block(at, q, blocks[b][0, :, cols], b, head)
            prob = jnp.exp(s - top) * inv
            probs[b] = prob
            dprob = nt(d_ctx, blocks[b][1, :, cols])
            dprobs[b] = dprob
            delta = delta + jnp.sum(prob * dprob, axis=1, keepdims=True)
        dq = jnp.zeros((ROWS, 128), F32)
        for b in range(8):
            prob = probs[b]
            d_score = (prob * (dprobs[b] - delta) * SCALE).astype(BF)
            dq = dq + nn(d_score, blocks[b][0, :, cols])
            dk = tn(d_score, q)
            dv = tn(prob.astype(BF), d_ctx)
            if b < 4:
                kept[b, 0, :, cols] = dk
                kept[b, 1, :, cols] = dv
            else:
                sent[b - 4, 0, :, cols] = dk.astype(BF)
                sent[b - 4, 1, :, cols] = dv.astype(BF)
        dq_out[:, cols] = (dq * table[0] - pltpu.roll(dq, 64, 1) * table[1]).astype(BF)


def small_kernel(at, x, rinv, low, ups, table, dq, own, one, two, three, out, grads, g_out):
    total = own[...] + one[...].astype(F32) + two[...].astype(F32) + three[...].astype(F32)
    grads[0] = dq[...]
    for h in range(2):
        cols = slice(h * 128, h * 128 + 128)
        v = total[0][:, cols]
        grads[1, :, cols] = (v * table[0] - pltpu.roll(v, 64, 1) * table[1]).astype(BF)
    grads[2] = total[1].astype(BF)
    pair = jnp.concatenate([grads[0], grads[2]], 1)
    g = nt(pair, ups[...])
    high = g.astype(BF)
    rest = g - high.astype(F32)
    middle = rest.astype(BF)
    low_part = (rest - middle.astype(F32)).astype(BF)
    g3 = jnp.concatenate([high, middle, low_part], 1)
    g_out[...] = g3
    scale = rinv[:, :1]
    for i in range(Z):
        normed = (x[i].astype(F32) * scale).astype(BF)
        r = tn(g3, normed)
        r = r[:16] + r[16:32] + r[32:48]
        for core in range(2):
            for x_place in range(2):
                at_col = (core * 2 + x_place) * 128
                out[i * 4 + x_place * 2 + core, :16, :] = r[:, at_col : at_col + 128]
    up = tn(low[...], pair)
    zero = jnp.zeros((7, 128), F32)
    for r in range(16):
        for half in range(2):
            col = half * 128 + (0 if r < 8 else 256)
            row = jnp.concatenate([up[r : r + 1, col : col + 128], zero], 0)
            out[2 * r + half, 16:24, :] = row


def unproject_kernel(at, x, rinv, down3, grads, g3, *refs):
    mine, theirs = refs[:9], refs[9:18]
    out = refs[18]
    z, core = place_of(at)
    head = at[4]
    scale = rinv[:, :1]
    rows = jnp.zeros((ROWS, 1), F32)
    for step in range(Z):
        here = chunk_at(z, step)
        to = lax.rem(here - head + Z, Z)
        for side, parity in ((mine, core), (theirs, 1 - core)):
            cols = columns(parity)
            acc = 2.0 * nn(g3[...], down3[here, :, cols])
            for j in range(3):
                acc = acc + nt(grads[j], weight(side, step, j))
            xn = x[here, :, cols].astype(F32) * scale
            rows = rows + jnp.sum(acc * xn, axis=1, keepdims=True)
            out[to, :ROWS, cols] = acc.astype(BF)
    flat = jnp.broadcast_to(rows, (ROWS, 128)).T[:16]
    high = flat.astype(BF)
    rest = (flat - high.astype(F32)).astype(BF)
    for k in range(Z):
        out[k, ROWS:, :256] = high
        out[k, ROWS:, 256:] = rest


def per_device(
    tokens, w_query, w_key, w_value, w_out, query_down, query_up, value_down, value_up, shifted, grad_out
):
    place = lax.axis_index("ctx")
    head_place = lax.axis_index("head")
    z, x_place, core = place // 4, (place // 2) % 2, place % 2
    seq_total = CTX * ROWS
    offsets = lax.dynamic_slice_in_dim(shifted, head_place * 2, 2) * 4
    spot = jnp.mod(place - offsets, 8)
    at = jnp.stack([z, core, spot[0], spot[1], head_place]).astype(jnp.int32)

    x8 = share(core_first(tokens))
    qkv_mine, qkv_theirs = ring(jnp.stack([w_query, w_key, w_value]), x_place)
    dy8 = share(core_first(grad_out))
    out_mine, out_theirs = ring(w_out.T[None], x_place)

    down = jnp.concatenate([query_down, value_down], 1)
    down = down.reshape(Z, 2, 2, 128, 16).transpose(0, 4, 2, 1, 3).reshape(Z, 16, 512)
    down3 = jnp.concatenate([down, down, down], 1)
    none = jnp.zeros_like(query_up)
    ups = jnp.concatenate(
        [jnp.concatenate([query_up, none], 1), jnp.concatenate([none, value_up], 1)], 0
    )
    positions = (place * ROWS + jnp.arange(ROWS, dtype=jnp.int32)).astype(F32)
    freq = jnp.power(10000.0, -jnp.arange(64, dtype=F32) * 2.0 / HEAD_DIM)
    angle = positions[:, None] * freq[None, :]
    cosine, sine = jnp.cos(angle), jnp.sin(angle)
    table = jnp.stack(
        [jnp.concatenate([cosine, cosine], 1), jnp.concatenate([-sine, sine], 1)]
    )

    query, keyval, rinv, low = whole(
        [((ROWS, 256), BF), ((2, ROWS, 256), BF), ((ROWS, 128), F32), ((ROWS, 16), BF)],
        22,
        project_kernel,
        [at, x8, down, ups, table, *qkv_mine, *qkv_theirs],
        [pltpu.VMEM((Z, ROWS, 512), BF)],
        flops=2 * 256 * 4096 * 768,
    )
    own = [keyval] + [chips(keyval, step) for step in (1, 2, 3)]
    blocks = own + [swap_core(block) for block in own]
    (d_context,) = whole(
        [((ROWS, 256), BF)],
        19,
        context_grad_kernel,
        [at, dy8, *out_mine, *out_theirs],
        flops=2 * 256 * 4096 * 256,
    )
    partial, stats = whole(
        [((Z, ROWS, 512), BF), ((4, ROWS, 128), F32)],
        27,
        forward_kernel,
        [at, query, *blocks, *out_mine, *out_theirs],
        [pltpu.VMEM((8, ROWS, ROWS), F32), pltpu.VMEM((ROWS, 256), BF)],
        flops=8 * 256 * 2048 * 128,
    )
    attn = jnp.sum(lax.all_to_all(partial, "head", 0, 0).astype(F32), axis=0)
    output = (tokens.astype(F32) + core_first(attn)).astype(BF)
    dq_pre, kept, sent = whole(
        [((ROWS, 256), BF), ((4, 2, ROWS, 256), F32), ((4, 2, ROWS, 256), BF)],
        12,
        backward_kernel,
        [at, query, d_context, table, stats, *blocks],
        [pltpu.VMEM((8, ROWS, ROWS), F32), pltpu.VMEM((8, ROWS, ROWS), F32)],
        flops=20 * 256 * 2048 * 128,
    )
    summed = kept + swap_core(sent).astype(F32)
    back = [chips(summed[step].astype(BF), step, True) for step in (1, 2, 3)]
    pieces, grads, g3 = whole(
        [((CTX, 24, 128), F32), ((3, ROWS, 256), BF), ((ROWS, 48), BF)],
        10,
        small_kernel,
        [at, x8, rinv, low, ups, table, dq_pre, summed[0], *back],
        flops=2 * 256 * 4096 * 48,
    )
    (terms,) = whole(
        [((Z, ROWS + 16, 512), BF)],
        23,
        unproject_kernel,
        [at, x8, rinv, down3, grads, g3, *qkv_mine, *qkv_theirs],
        flops=2 * 256 * 4096 * 768,
    )
    got = terms[0].astype(F32)
    for step in range(1, HEAD):
        got = got + move(terms[step], "head", HEAD, lambda i: (i + step) % HEAD).astype(F32)
    row_mean = (got[ROWS, :256] + got[ROWS, 256:])[:, None] / 4096.0
    scale = rinv[:, :1]
    x_own = tokens.astype(F32) * scale
    grad_tokens = (
        grad_out.astype(F32) + scale * (core_first(got[:ROWS]) - x_own * row_mean)
    ).astype(BF)

    scale_out = 2.0 / seq_total**0.5
    first = jnp.sum(lax.all_to_all(pieces, "ctx", 0, 0), axis=0) * scale_out
    second = jnp.sum(share(first[:16]), axis=0)
    third = jnp.concatenate([second, first[16:]], 0)
    third = lax.all_to_all(jnp.broadcast_to(third[None], (CTX, 24, 128)), "ctx", 0, 0)
    down_all = third[:, :16].transpose(0, 2, 1).reshape(4096, 16)
    up_all = third[:, 16].reshape(16, 256)
    return (output, grad_tokens, down_all[:, :8], up_all[:8], down_all[:, 8:], up_all[8:])


def solution(mesh):
    in_specs = (
        P("ctx", "head"),
        P("ctx", "head"),
        P("ctx", "head"),
        P("ctx", "head"),
        P("head", "ctx"),
        P(),
        P(None, "head"),
        P(),
        P(None, "head"),
        P(),
        P("ctx", "head"),
    )
    out_specs = (P("ctx", "head"), P("ctx", "head"), P(), P(None, "head"), P(), P(None, "head"))
    return jax.shard_map(
        per_device, mesh=mesh, in_specs=in_specs, out_specs=out_specs, check_vma=False
    )
```

```python
import jax
import jax.numpy as jnp
from jax import lax
from jax.experimental import pallas as pl
from jax.experimental.pallas import tpu as pltpu
from jax.sharding import PartitionSpec as P

HEAD_DIM = 128
BF = jnp.bfloat16
F32 = jnp.float32
CTX = 32
HEAD = 8
Z = 8
ROWS = 256
SCALE = 1.0 / HEAD_DIM**0.5
HIDDEN = -1e30
DELTA = (0, -1, 1, -2, 2, -3, 3, 4)
VMEM_LIMIT = 24 * 1024 * 1024


def move(value, axis, count, to):
    return lax.ppermute(value, axis, [(i, to(i)) for i in range(count)])


def swap_core(value):
    return move(value, "ctx", CTX, lambda i: i ^ 1)


def swap_x(value):
    return move(value, "ctx", CTX, lambda i: i ^ 2)


def along_z(value, step):
    return move(value, "ctx", CTX, lambda i: (i + 4 * step) % CTX)


def chips(value, step, back=False):
    pairs = [(i, (i + 2 * step) % CTX) for i in range(CTX)]
    if step == 3:
        pairs = [p for p in pairs if (p[1] // 2) % 2 == 1]
    if back:
        pairs = [(d, s) for s, d in pairs]
    return lax.ppermute(value, "ctx", pairs)


def core_first(value):
    lead = value.shape[:-1]
    return value.reshape(*lead, 2, 2, 128).swapaxes(-3, -2).reshape(*lead, 512)


def ring(pack, other, x_place):
    block = jnp.where(
        x_place == 0,
        jnp.concatenate([pack, other], 1),
        jnp.concatenate([other, pack], 1),
    )
    up = down = block
    parts = [block]
    for _ in range(3):
        up = along_z(up, 1)
        down = along_z(down, -1)
        parts += [up, down]
    half = block.shape[1] // 2
    parts += [along_z(up[:, :half], 1), along_z(down[:, half:], -1)]
    return parts + [swap_core(p) for p in parts]


def after(value, other):
    return lax.optimization_barrier((value, other))[0]


def share(value):
    sent = jnp.broadcast_to(value[None], (HEAD,) + value.shape)
    return lax.all_to_all(sent, "head", 0, 0)


def nn(a, b):
    return jnp.dot(a, b, preferred_element_type=F32)


def nt(a, b):
    return lax.dot_general(a, b, (((1,), (1,)), ((), ())), preferred_element_type=F32)


def tn(a, b):
    return lax.dot_general(a, b, (((0,), (0,)), ((), ())), preferred_element_type=F32)


def part_spec(start, count, rows):
    return pl.BlockSpec(
        (count, rows, 256), lambda i: (start // count, 0, 0), pipeline_mode=pl.Buffered(1)
    )


def whole(shape_dtypes, kernel, args, weights=None, scratch=(), flops=0):
    args = list(args)
    specs = [pl.BlockSpec(memory_space=pltpu.SMEM)] * 2
    specs += [pl.BlockSpec(memory_space=pltpu.VMEM)] * (len(args) - 2)
    if weights is not None:
        parts, start, count = weights
        full, half = part_spec(start, count, 256), part_spec(start, count, 128)
        args += parts
        specs += ([full] * 7 + [half] * 2) * 2
    moved = sum(a.size * a.dtype.itemsize for a in args)
    return pl.pallas_call(
        kernel,
        grid=(1,),
        out_shape=[jax.ShapeDtypeStruct(s, d) for s, d in shape_dtypes],
        in_specs=specs,
        out_specs=[pl.BlockSpec(memory_space=pltpu.VMEM)] * len(shape_dtypes),
        scratch_shapes=list(scratch),
        compiler_params=pltpu.CompilerParams(vmem_limit_bytes=VMEM_LIMIT),
        cost_estimate=pl.CostEstimate(flops=flops, bytes_accessed=moved, transcendentals=0),
    )(*args)


def place_of(at):
    place = at[0]
    return place // 4, lax.rem(place, 2)


def chunk_at(z, step):
    return lax.rem(z + (DELTA[step] + Z), Z)


def columns(core):
    return pl.ds(pl.multiple_of(core * 256, 256), 256)


def weight(mine, step, j):
    if step < 7:
        return mine[step][j]
    return jnp.concatenate([mine[7][j], mine[8][j]], 0)


def turn(v, table):
    return v * table[0] + pltpu.roll(v, 64, 1) * table[1]


def project_kernel(at, shifted, x, down, ups, table, *refs):
    mine, theirs = refs[:9], refs[9:18]
    query, keyval, rinv_out, low_out, normed = refs[18:]
    z, core = place_of(at)
    total = jnp.zeros((ROWS, 1), F32)
    for i in range(Z):
        part = x[i].astype(F32)
        total = total + jnp.sum(part * part, axis=1, keepdims=True)
    rinv = lax.rsqrt(total / 4096.0 + 1e-05)
    rinv_out[...] = jnp.broadcast_to(rinv, (ROWS, 128))
    low = jnp.zeros((ROWS, 16), F32)
    for i in range(Z):
        rounded = (x[i].astype(F32) * rinv).astype(BF)
        normed[i] = rounded
        rows = [down[pl.ds(i * 512 + a, 128), :] for a in (0, 256, 128, 384)]
        low = low + nn(rounded, jnp.concatenate(rows, 0))[:, :16]
    low = low.astype(BF)
    low_out[...] = low
    acc = [jnp.zeros((ROWS, 256), F32) for _ in range(3)]
    for step in range(Z):
        here = chunk_at(z, step)
        for side, parity in ((mine, core), (theirs, 1 - core)):
            a = normed[here, :, columns(parity)]
            for j in range(3):
                acc[j] = acc[j] + nn(a, weight(side, step, j))
    extra = 2.0 * nn(low, ups[...])
    q_lin = acc[0] + extra[:, :256]
    for h in range(2):
        cols = slice(h * 128, h * 128 + 128)
        query[:, cols] = turn(q_lin[:, cols], table).astype(BF)
        keyval[0, :, cols] = turn(acc[1][:, cols], table).astype(BF)
    keyval[1] = (acc[2] + extra[:, 256:]).astype(BF)


def context_grad_kernel(at, shifted, dy, *refs):
    mine, theirs = refs[:9], refs[9:18]
    out = refs[18]
    z, core = place_of(at)
    acc = jnp.zeros((ROWS, 256), F32)
    for step in range(Z):
        here = chunk_at(z, step)
        for side, parity in ((mine, core), (theirs, 1 - core)):
            acc = acc + nn(dy[here, :, columns(parity)], weight(side, step, 0))
    out[...] = acc.astype(BF)


def score_block(at, shifted, q, key, b, head):
    core = lax.rem(at[0], 2)
    spot = lax.rem(at[0] + 8 - 4 * shifted[2 * at[1] + head], 8)
    s = nt(q, key) * SCALE
    if b == 0:
        row = lax.broadcasted_iota(jnp.int32, (ROWS, ROWS), 0)
        col = lax.broadcasted_iota(jnp.int32, (ROWS, ROWS), 1)
        return jnp.where(col <= row, s, HIDDEN)
    behind = 2 * b if b < 4 else 2 * (b - 4) + 2 * core - 1
    seen = jnp.logical_and(behind > 0, behind <= spot)
    return s + jnp.where(seen, 0.0, HIDDEN)


def attention_kernel(at, shifted, query, d_context, table, *refs):
    blocks, mine, theirs = refs[:8], refs[8:17], refs[17:26]
    out, dq_out, kept, sent, probs, dprobs, context = refs[26:]
    z, core = place_of(at)
    for head in range(2):
        cols = slice(head * 128, head * 128 + 128)
        q = query[:, cols]
        d_ctx = d_context[:, cols]
        top = jnp.full((ROWS, 1), HIDDEN, F32)
        for b in range(8):
            s = score_block(at, shifted, q, blocks[b][0, :, cols], b, head)
            probs[b] = s
            top = jnp.maximum(top, jnp.max(s, axis=1, keepdims=True))
        total = jnp.zeros((ROWS, 1), F32)
        for b in range(8):
            e = jnp.exp(probs[b] - top)
            probs[b] = e
            total = total + jnp.sum(e, axis=1, keepdims=True)
        inv = 1.0 / total
        acc = jnp.zeros((ROWS, 128), F32)
        delta = jnp.zeros((ROWS, 1), F32)
        for b in range(8):
            prob = probs[b] * inv
            probs[b] = prob
            rounded = prob.astype(BF)
            value = blocks[b][1, :, cols]
            acc = acc + nn(rounded, value)
            dv = tn(rounded, d_ctx)
            dprob = nt(d_ctx, value)
            dprobs[b] = dprob
            delta = delta + jnp.sum(prob * dprob, axis=1, keepdims=True)
            if b < 4:
                kept[b, 1, :, cols] = dv
            else:
                sent[b - 4, 1, :, cols] = dv.astype(BF)
        context[:, cols] = acc.astype(BF)
        dq = jnp.zeros((ROWS, 128), F32)
        for b in range(8):
            d_score = (probs[b] * (dprobs[b] - delta) * SCALE).astype(BF)
            dq = dq + nn(d_score, blocks[b][0, :, cols])
            dk = tn(d_score, q)
            if b < 4:
                kept[b, 0, :, cols] = dk
            else:
                sent[b - 4, 0, :, cols] = dk.astype(BF)
        dq_out[:, cols] = (dq * table[0] - pltpu.roll(dq, 64, 1) * table[1]).astype(BF)
    for step in range(Z):
        here = chunk_at(z, step)
        for side, parity in ((mine, core), (theirs, 1 - core)):
            out[here, :, columns(parity)] = nt(context[...], weight(side, step, 0)).astype(BF)


def natural(v):
    return jnp.concatenate([v[:, :128], v[:, 256:384], v[:, 128:256], v[:, 384:]], 1)


def output_kernel(at, shifted, terms, tokens, out):
    total = terms[0].astype(F32)
    for i in range(1, HEAD):
        total = total + terms[i].astype(F32)
    out[...] = (tokens[...].astype(F32) + natural(total)).astype(BF)


def finish_kernel(at, shifted, tokens, grad_out, rinv, *refs):
    out = refs[-1]
    total = refs[0][0].astype(F32)
    for other in refs[1:-1]:
        total = total + other[...].astype(F32)
    sums = total[ROWS : ROWS + 8]
    sums = sums[:, :ROWS] + sums[:, ROWS:]
    row_mean = jnp.concatenate([sums] * 16, 0).T[:, :1] / 4096.0
    scale = rinv[:, :1]
    x_own = tokens[...].astype(F32) * scale
    out[...] = (
        grad_out[...].astype(F32) + scale * (natural(total[:ROWS]) - x_own * row_mean)
    ).astype(BF)


def small_kernel(at, shifted, x, rinv, low, ups, table, dq, own, one, two, three, out, grads, g_out):
    total = own[...] + one[...].astype(F32) + two[...].astype(F32) + three[...].astype(F32)
    grads[0] = dq[...]
    for h in range(2):
        cols = slice(h * 128, h * 128 + 128)
        v = total[0][:, cols]
        grads[1, :, cols] = (v * table[0] - pltpu.roll(v, 64, 1) * table[1]).astype(BF)
    grads[2] = total[1].astype(BF)
    pair = jnp.concatenate([grads[0], grads[2]], 1)
    g = nt(pair, ups[...])
    high = g.astype(BF)
    rest = g - high.astype(F32)
    middle = rest.astype(BF)
    low_part = (rest - middle.astype(F32)).astype(BF)
    g3 = jnp.concatenate([high, middle, low_part], 1)
    g_out[...] = g3
    scale = rinv[:, :1]
    for i in range(Z):
        normed = (x[i].astype(F32) * scale).astype(BF)
        r = tn(g3, normed)
        r = r[:16] + r[16:32] + r[32:48]
        for core in range(2):
            for x_place in range(2):
                at_col = (core * 2 + x_place) * 128
                out[i * 4 + x_place * 2 + core, :16, :] = r[:, at_col : at_col + 128]
    up = tn(low[...], pair)
    zero = jnp.zeros((7, 128), F32)
    for r in range(16):
        for half in range(2):
            col = half * 128 + (0 if r < 8 else 256)
            row = jnp.concatenate([up[r : r + 1, col : col + 128], zero], 0)
            out[2 * r + half, 16:24, :] = row


def unproject_kernel(at, shifted, x, rinv, down, grads, g3, *refs):
    mine, theirs = refs[:9], refs[9:18]
    out = refs[18]
    z, core = place_of(at)
    head = at[1]
    scale = rinv[:, :1]
    rows = jnp.zeros((ROWS, 1), F32)
    for step in range(Z):
        here = chunk_at(z, step)
        to = lax.rem(here - head + Z, Z)
        for side, parity in ((mine, core), (theirs, 1 - core)):
            cols = columns(parity)
            start = here * 512 + parity * 128
            rows_of = [down[pl.ds(pl.multiple_of(start + a, 128), 128), :] for a in (0, 256)]
            acc = 2.0 * nt(g3[...], jnp.concatenate(rows_of, 0))
            for j in range(3):
                acc = acc + nt(grads[j], weight(side, step, j))
            xn = x[here, :, cols].astype(F32) * scale
            rows = rows + jnp.sum(acc * xn, axis=1, keepdims=True)
            out[to, :ROWS, cols] = acc.astype(BF)
    flat = jnp.broadcast_to(rows, (ROWS, 128)).T[:16]
    high = flat.astype(BF)
    rest = (flat - high.astype(F32)).astype(BF)
    for k in range(Z):
        out[k, ROWS:, :256] = high
        out[k, ROWS:, 256:] = rest


def per_device(
    tokens, w_query, w_key, w_value, w_out, query_down, query_up, value_down, value_up, shifted, grad_out
):
    place = lax.axis_index("ctx")
    head_place = lax.axis_index("head")
    x_place = (place // 2) % 2
    seq_total = CTX * ROWS
    at = jnp.stack([place, head_place]).astype(jnp.int32)

    pack = jnp.stack([w_query, w_key, w_value, w_out.T])
    other = swap_x(pack)
    parts = ring(pack, other, x_place)
    x8 = share(after(core_first(tokens), parts[1]))
    dy8 = share(after(core_first(grad_out), x8))

    down = jnp.concatenate([query_down, value_down] * 3, 1)
    none = jnp.zeros_like(query_up)
    ups = jnp.concatenate(
        [jnp.concatenate([query_up, none], 1), jnp.concatenate([none, value_up], 1)], 0
    )
    positions = (place * ROWS + jnp.arange(ROWS, dtype=jnp.int32)).astype(F32)
    freq = jnp.power(10000.0, -jnp.arange(64, dtype=F32) * 2.0 / HEAD_DIM)
    angle = positions[:, None] * freq[None, :]
    cosine, sine = jnp.cos(angle), jnp.sin(angle)
    table = jnp.stack(
        [jnp.concatenate([cosine, cosine], 1), jnp.concatenate([-sine, sine], 1)]
    )

    query, keyval, rinv, low = whole(
        [((ROWS, 256), BF), ((2, ROWS, 256), BF), ((ROWS, 128), F32), ((ROWS, 16), BF)],
        project_kernel,
        [at, shifted, x8, down, ups, table],
        (parts, 0, 3),
        [pltpu.VMEM((Z, ROWS, 512), BF)],
        flops=2 * 256 * 4096 * 768,
    )
    own = [keyval] + [chips(keyval, step) for step in (1, 2, 3)]
    blocks = own + [swap_core(block) for block in own]
    (d_context,) = whole(
        [((ROWS, 256), BF)],
        context_grad_kernel,
        [at, shifted, dy8],
        (parts, 3, 1),
        flops=2 * 256 * 4096 * 256,
    )
    partial, dq_pre, kept, sent = whole(
        [
            ((Z, ROWS, 512), BF),
            ((ROWS, 256), BF),
            ((4, 2, ROWS, 256), F32),
            ((4, 2, ROWS, 256), BF),
        ],
        attention_kernel,
        [at, shifted, query, d_context, table, *blocks],
        (parts, 3, 1),
        [
            pltpu.VMEM((8, ROWS, ROWS), F32),
            pltpu.VMEM((8, ROWS, ROWS), F32),
            pltpu.VMEM((ROWS, 256), BF),
        ],
        flops=24 * 256 * 2048 * 128,
    )
    attn = lax.all_to_all(partial, "head", 0, 0)
    summed = kept + swap_core(sent).astype(F32)
    back = [chips(summed[step].astype(BF), step, True) for step in (1, 2, 3)]
    pieces, grads, g3 = whole(
        [((CTX, 24, 128), F32), ((3, ROWS, 256), BF), ((ROWS, 48), BF)],
        small_kernel,
        [at, shifted, x8, rinv, low, ups, table, dq_pre, summed[0], *back],
        flops=2 * 256 * 4096 * 48,
    )
    (terms,) = whole(
        [((Z, ROWS + 16, 512), BF)],
        unproject_kernel,
        [at, shifted, x8, rinv, down, grads, g3],
        (parts, 0, 3),
        flops=2 * 256 * 4096 * 768,
    )
    (output,) = whole([((ROWS, 512), BF)], output_kernel, [at, shifted, attn, tokens])
    scale_out = 2.0 / seq_total**0.5
    first = jnp.sum(lax.all_to_all(after(pieces, attn), "ctx", 0, 0), axis=0) * scale_out
    got = [
        move(terms[step], "head", HEAD, lambda i: (i + step) % HEAD) for step in range(1, HEAD)
    ]
    (grad_tokens,) = whole(
        [((ROWS, 512), BF)],
        finish_kernel,
        [at, shifted, tokens, grad_out, rinv, terms[:1], *got],
    )
    second = jnp.sum(share(after(first, got[:2])[:16]), axis=0)
    third = after(jnp.concatenate([second, first[16:]], 0), got[2:5])
    third = lax.all_to_all(jnp.broadcast_to(third[None], (CTX, 24, 128)), "ctx", 0, 0)
    down_all = third[:, :16].transpose(0, 2, 1).reshape(4096, 16)
    up_all = third[:, 16].reshape(16, 256)
    return (output, grad_tokens, down_all[:, :8], up_all[:8], down_all[:, 8:], up_all[8:])


def solution(mesh):
    in_specs = (
        P("ctx", "head"),
        P("ctx", "head"),
        P("ctx", "head"),
        P("ctx", "head"),
        P("head", "ctx"),
        P(),
        P(None, "head"),
        P(),
        P(None, "head"),
        P(),
        P("ctx", "head"),
    )
    out_specs = (P("ctx", "head"), P("ctx", "head"), P(), P(None, "head"), P(), P(None, "head"))
    return jax.shard_map(
        per_device, mesh=mesh, in_specs=in_specs, out_specs=out_specs, check_vma=False
    )
```

```python
import jax
import jax.numpy as jnp
from jax import lax
from jax.experimental import pallas as pl
from jax.experimental.pallas import tpu as pltpu
from jax.sharding import PartitionSpec as P

HEAD_DIM = 128
BF = jnp.bfloat16
F32 = jnp.float32
CTX = 32
HEAD = 8
Z = 8
ROWS = 256
SCALE = 1.0 / HEAD_DIM**0.5
HIDDEN = -1e30
DELTA = (0, -1, 1, -2, 2, -3, 3, 4)
VMEM_LIMIT = 60 * 1024 * 1024


def move(value, axis, count, to):
    return lax.ppermute(value, axis, [(i, to(i)) for i in range(count)])


def swap_core(value):
    return move(value, "ctx", CTX, lambda i: i ^ 1)


def swap_x(value):
    return move(value, "ctx", CTX, lambda i: i ^ 2)


def along_z(value, step):
    return move(value, "ctx", CTX, lambda i: (i + 4 * step) % CTX)


def chips(value, step, back=False):
    pairs = [(i, (i + 2 * step) % CTX) for i in range(CTX)]
    if step == 3:
        pairs = [p for p in pairs if (p[1] // 2) % 2 == 1]
    if back:
        pairs = [(d, s) for s, d in pairs]
    return lax.ppermute(value, "ctx", pairs)


def ring(pack, other, x_place):
    block = jnp.where(
        x_place == 0,
        jnp.concatenate([pack, other], 1),
        jnp.concatenate([other, pack], 1),
    )
    up = down = block
    parts = [block]
    for _ in range(3):
        up = along_z(up, 1)
        down = along_z(down, -1)
        parts += [up, down]
    half = block.shape[1] // 2
    parts += [along_z(up[:, :half], 1), along_z(down[:, half:], -1)]
    return parts + [swap_core(p) for p in parts]


def after(value, other):
    return lax.optimization_barrier((value, other))[0]


def share(value):
    sent = jnp.broadcast_to(value[None], (HEAD,) + value.shape)
    return lax.all_to_all(sent, "head", 0, 0)


def nn(a, b):
    return jnp.dot(a, b, preferred_element_type=F32)


def nt(a, b):
    return lax.dot_general(a, b, (((1,), (1,)), ((), ())), preferred_element_type=F32)


def tn(a, b):
    return lax.dot_general(a, b, (((0,), (0,)), ((), ())), preferred_element_type=F32)


def part_spec(start, count, rows):
    return pl.BlockSpec(
        (count, rows, 256), lambda i: (start // count, 0, 0), pipeline_mode=pl.Buffered(1)
    )


def whole(shape_dtypes, kernel, args, weights=None, leading=(), scratch=(), flops=0):
    args = list(args)
    specs = [pl.BlockSpec(memory_space=pltpu.VMEM)] * len(args)
    for array in leading:
        args.append(array)
        rank = array.ndim
        specs.append(
            pl.BlockSpec(
                (1,) + array.shape[1:],
                lambda i, rank=rank: (0,) * rank,
                pipeline_mode=pl.Buffered(1),
            )
        )
    if weights is not None:
        parts, start, count = weights
        full, half = part_spec(start, count, 256), part_spec(start, count, 128)
        args += parts
        specs += ([full] * 7 + [half] * 2) * 2
    moved = sum(a.size * a.dtype.itemsize for a in args)
    return pl.pallas_call(
        kernel,
        grid=(1,),
        out_shape=[jax.ShapeDtypeStruct(s, d) for s, d in shape_dtypes],
        in_specs=specs,
        out_specs=[pl.BlockSpec(memory_space=pltpu.VMEM)] * len(shape_dtypes),
        scratch_shapes=list(scratch),
        compiler_params=pltpu.CompilerParams(vmem_limit_bytes=VMEM_LIMIT),
        cost_estimate=pl.CostEstimate(flops=flops, bytes_accessed=moved, transcendentals=0),
    )(*args)


def place_of():
    place = lax.axis_index("ctx")
    return place // 4, lax.rem(place, 2)


def head_of():
    place = lax.axis_index("head")
    return place // 4, lax.rem(place, 4)


def chunk_at(z, step):
    return lax.rem(z + (DELTA[step] + Z), Z)


def columns(core):
    return pl.ds(pl.multiple_of(core * 256, 256), 256)


def weight(mine, step, j):
    if step < 7:
        return mine[step][j]
    return jnp.concatenate([mine[7][j], mine[8][j]], 0)


def turn(v, table):
    return v * table[0] + pltpu.roll(v, 64, 1) * table[1]


def natural(v):
    return jnp.concatenate([v[:, :128], v[:, 256:384], v[:, 128:256], v[:, 384:]], 1)


def pack_kernel(w_query, w_key, w_value, w_out, pack):
    pack[0] = w_query[...]
    pack[1] = w_key[...]
    pack[2] = w_value[...]
    pack[3] = w_out[...].astype(F32).T.astype(BF)


def order_kernel(tokens, grad_out, x, dy):
    x[...] = natural(tokens[...])
    dy[...] = natural(grad_out[...])


def down_rows(array, start):
    return jnp.concatenate([array[pl.ds(start + a, 128), :] for a in (0, 256, 128, 384)], 0)


def chunk_of(k, x_low):
    return x_low * 4 + lax.rem(head_of()[1] + 4 - k, 4)


def project_kernel(down_q, down_v, ups, table, *refs):
    got, mine, theirs = refs[:4], refs[4:13], refs[13:22]
    query, keyval, rinv_out, low_out, x_out, normed = refs[22:]
    z, core = place_of()
    total = jnp.zeros((ROWS, 1), F32)
    for k in range(4):
        for x_low in range(2):
            raw = got[k][x_low]
            x_out[chunk_of(k, x_low)] = raw
            part = raw.astype(F32)
            total = total + jnp.sum(part * part, axis=1, keepdims=True)
    rinv = lax.rsqrt(total / 4096.0 + 1e-05)
    rinv_out[...] = jnp.broadcast_to(rinv, (ROWS, 128))
    low_q = jnp.zeros((ROWS, 8), F32)
    low_v = jnp.zeros((ROWS, 8), F32)
    for i in range(Z):
        rounded = (x_out[i].astype(F32) * rinv).astype(BF)
        normed[i] = rounded
        low_q = low_q + nn(rounded, down_rows(down_q, i * 512))
        low_v = low_v + nn(rounded, down_rows(down_v, i * 512))
    low = jnp.concatenate([low_q, low_v], 1).astype(BF)
    low_out[...] = low
    acc = [jnp.zeros((ROWS, 256), F32) for _ in range(3)]
    for step in range(Z):
        here = chunk_at(z, step)
        for side, parity in ((mine, core), (theirs, 1 - core)):
            a = normed[here, :, columns(parity)]
            for j in range(3):
                acc[j] = acc[j] + nn(a, weight(side, step, j))
    extra = 2.0 * nn(low, ups[...])
    q_lin = acc[0] + extra[:, :256]
    for h in range(2):
        cols = slice(h * 128, h * 128 + 128)
        query[:, cols] = turn(q_lin[:, cols], table).astype(BF)
        keyval[0, :, cols] = turn(acc[1][:, cols], table).astype(BF)
    keyval[1] = (acc[2] + extra[:, 256:]).astype(BF)


def context_grad_kernel(down_q, down_v, *refs):
    got, mine, theirs = refs[:4], refs[4:13], refs[13:22]
    out, down, dy = refs[22:]
    z, core = place_of()
    for k in range(4):
        for x_low in range(2):
            dy[chunk_of(k, x_low)] = got[k][x_low]
    acc = jnp.zeros((ROWS, 256), F32)
    for step in range(Z):
        here = chunk_at(z, step)
        for side, parity in ((mine, core), (theirs, 1 - core)):
            acc = acc + nn(dy[here, :, columns(parity)], weight(side, step, 0))
    out[...] = acc.astype(BF)
    pair = [down_q[...].astype(F32), down_v[...].astype(F32)]
    down[...] = jnp.concatenate(pair * 3, 1).astype(BF)


def score_block(spots, q, key, b, head):
    core = place_of()[1]
    spot = spots[head : head + 1, :1]
    s = nt(q, key) * SCALE
    if b == 0:
        row = lax.broadcasted_iota(jnp.int32, (ROWS, ROWS), 0)
        col = lax.broadcasted_iota(jnp.int32, (ROWS, ROWS), 1)
        return jnp.where(col <= row, s, HIDDEN)
    behind = 2 * b if b < 4 else 2 * (b - 4) + 2 * core - 1
    if b == 4:
        return s + jnp.where(jnp.logical_and(spot >= behind, spot * 0 < behind), 0.0, HIDDEN)
    return s + jnp.where(spot >= behind, 0.0, HIDDEN)


def attention_kernel(spots, query, d_context, table, *refs):
    blocks, mine, theirs = refs[:8], refs[8:17], refs[17:26]
    out, dq_out, first, kept, sent, probs, dprobs, context = refs[26:]
    z, core = place_of()
    for head in range(2):
        cols = slice(head * 128, head * 128 + 128)
        q = query[:, cols]
        d_ctx = d_context[:, cols]
        top = jnp.full((ROWS, 1), HIDDEN, F32)
        for b in range(8):
            s = score_block(spots, q, blocks[b][0, :, cols], b, head)
            probs[b] = s
            top = jnp.maximum(top, jnp.max(s, axis=1, keepdims=True))
        total = jnp.zeros((ROWS, 1), F32)
        for b in range(8):
            e = jnp.exp(probs[b] - top)
            probs[b] = e
            total = total + jnp.sum(e, axis=1, keepdims=True)
        inv = 1.0 / total
        acc = jnp.zeros((ROWS, 128), F32)
        delta = jnp.zeros((ROWS, 1), F32)
        for b in range(8):
            prob = probs[b] * inv
            probs[b] = prob
            rounded = prob.astype(BF)
            value = blocks[b][1, :, cols]
            acc = acc + nn(rounded, value)
            dv = tn(rounded, d_ctx)
            dprob = nt(d_ctx, value)
            dprobs[b] = dprob
            delta = delta + jnp.sum(prob * dprob, axis=1, keepdims=True)
            if b == 0:
                first[1, :, cols] = dv
            elif b < 4:
                kept[b - 1, 1, :, cols] = dv.astype(BF)
            else:
                sent[b - 4, 1, :, cols] = dv.astype(BF)
        context[:, cols] = acc.astype(BF)
        dq = jnp.zeros((ROWS, 128), F32)
        for b in range(8):
            d_score = (probs[b] * (dprobs[b] - delta) * SCALE).astype(BF)
            dq = dq + nn(d_score, blocks[b][0, :, cols])
            dk = tn(d_score, q)
            if b == 0:
                first[0, :, cols] = dk
            elif b < 4:
                kept[b - 1, 0, :, cols] = dk.astype(BF)
            else:
                sent[b - 4, 0, :, cols] = dk.astype(BF)
        dq_out[:, cols] = (dq * table[0] - pltpu.roll(dq, 64, 1) * table[1]).astype(BF)
    y = head_of()[1]
    for step in range(Z):
        here = chunk_at(z, step)
        x_low, to = here // 4, lax.rem(lax.rem(here, 4) - y + 4, 4)
        for side, parity in ((mine, core), (theirs, 1 - core)):
            out[to, x_low, :, columns(parity)] = nt(context[...], weight(side, step, 0)).astype(BF)


def combine_kernel(first, kept, other, own, one, two, three):
    own[...] = first[...] + other[0].astype(F32)
    for t, out in enumerate((one, two, three)):
        out[...] = (kept[t].astype(F32) + other[t + 1].astype(F32)).astype(BF)


def along_y_kernel(one, two, three, mine, keep, send):
    x_low = head_of()[0]
    count = keep.shape[0]

    def total(at):
        parts = [mine[0, at], one[at], two[at], three[at]]
        result = parts[0].astype(F32)
        for part in parts[1:]:
            result = result + part.astype(F32)
        return result

    here, there = total(x_low), total(1 - x_low)
    keep[...] = here
    send[:ROWS] = there[:ROWS].astype(BF)
    if count > ROWS:
        sums = there[ROWS:, :ROWS] + there[ROWS:, ROWS:]
        high = sums.astype(BF)
        send[ROWS:, :ROWS] = high
        send[ROWS:, ROWS:] = (sums - high.astype(F32)).astype(BF)


def output_kernel(keep, got, tokens, out):
    total = keep[...] + got[...].astype(F32)
    out[...] = (tokens[...].astype(F32) + natural(total)).astype(BF)


def finish_kernel(tokens, grad_out, rinv, keep, got, out):
    total = keep[...] + got[...].astype(F32)
    sums = total[ROWS : ROWS + 8]
    sums = sums[:, :ROWS] + sums[:, ROWS:]
    row_mean = jnp.concatenate([sums] * 16, 0).T[:, :1] / 4096.0
    scale = rinv[:, :1]
    x_own = tokens[...].astype(F32) * scale
    out[...] = (
        grad_out[...].astype(F32) + scale * (natural(total[:ROWS]) - x_own * row_mean)
    ).astype(BF)


def spread_kernel(third, down_q, down_v, up_q, up_v):
    for c in range(CTX):
        turned = third[c, :16].T
        down_q[c * 128 : c * 128 + 128, :] = turned[:, :8]
        down_v[c * 128 : c * 128 + 128, :] = turned[:, 8:]
        out, row = (up_q, c // 2) if c < 16 else (up_v, c // 2 - 8)
        half = (c % 2) * 128
        out[row : row + 1, half : half + 128] = third[c, 16:17]


def small_kernel(x, rinv, low, ups, table, dq, own, one, two, three, out, grads, g_out):
    total = own[...] + one[...].astype(F32) + two[...].astype(F32) + three[...].astype(F32)
    grads[0] = dq[...]
    for h in range(2):
        cols = slice(h * 128, h * 128 + 128)
        v = total[0][:, cols]
        grads[1, :, cols] = (v * table[0] - pltpu.roll(v, 64, 1) * table[1]).astype(BF)
    grads[2] = total[1].astype(BF)
    pair = jnp.concatenate([grads[0], grads[2]], 1)
    g = nt(pair, ups[...])
    high = g.astype(BF)
    rest = g - high.astype(F32)
    middle = rest.astype(BF)
    low_part = (rest - middle.astype(F32)).astype(BF)
    g3 = jnp.concatenate([high, middle, low_part], 1)
    g_out[...] = g3
    scale = rinv[:, :1]
    for i in range(Z):
        normed = (x[i].astype(F32) * scale).astype(BF)
        r = tn(g3, normed)
        r = r[:16] + r[16:32] + r[32:48]
        for core in range(2):
            for x_place in range(2):
                at_col = (core * 2 + x_place) * 128
                out[i * 4 + x_place * 2 + core, :16, :] = r[:, at_col : at_col + 128]
    up = tn(low[...], pair)
    zero = jnp.zeros((7, 128), F32)
    for r in range(16):
        for half in range(2):
            col = half * 128 + (0 if r < 8 else 256)
            row = jnp.concatenate([up[r : r + 1, col : col + 128], zero], 0)
            out[2 * r + half, 16:24, :] = row


def unproject_kernel(x, rinv, down, grads, g3, *refs):
    mine, theirs = refs[:9], refs[9:18]
    out = refs[18]
    z, core = place_of()
    y = head_of()[1]
    scale = rinv[:, :1]
    rows = jnp.zeros((ROWS, 1), F32)
    for step in range(Z):
        here = chunk_at(z, step)
        x_low, to = here // 4, lax.rem(lax.rem(here, 4) - y + 4, 4)
        for side, parity in ((mine, core), (theirs, 1 - core)):
            cols = columns(parity)
            start = here * 512 + parity * 128
            rows_of = [down[pl.ds(pl.multiple_of(start + a, 128), 128), :] for a in (0, 256)]
            acc = 2.0 * nt(g3[...], jnp.concatenate(rows_of, 0))
            for j in range(3):
                acc = acc + nt(grads[j], weight(side, step, j))
            xn = x[here, :, cols].astype(F32) * scale
            rows = rows + jnp.sum(acc * xn, axis=1, keepdims=True)
            out[to, x_low, :ROWS, cols] = acc.astype(BF)
    flat = jnp.broadcast_to(rows, (ROWS, 128)).T[:16]
    high = flat.astype(BF)
    rest = (flat - high.astype(F32)).astype(BF)
    for k in range(4):
        for x_low in range(2):
            out[k, x_low, ROWS:, :256] = high
            out[k, x_low, ROWS:, 256:] = rest


def swap_low(value):
    return move(value, "head", HEAD, lambda i: i ^ 4)


def along_y(value, step):
    return move(value, "head", HEAD, lambda i: (i // 4) * 4 + (i + step) % 4)


def gather_head(value, x_low):
    other = swap_low(value)
    both = jnp.where(x_low == 0, jnp.stack([value, other]), jnp.stack([other, value]))
    return [both] + [along_y(both, step) for step in (1, 2, 3)]


def sum_head(terms, hold=None):
    rows = terms.shape[2]
    sent = terms if hold is None else after(terms, hold)
    got = [along_y(sent[step], step) for step in (1, 2, 3)]
    keep, send = whole(
        [((rows, 512), F32), ((rows, 512), BF)], along_y_kernel, got, leading=[terms]
    )
    return got, keep, swap_low(send)


def per_device(
    tokens, w_query, w_key, w_value, w_out, query_down, query_up, value_down, value_up, shifted, grad_out
):
    place = lax.axis_index("ctx")
    head_place = lax.axis_index("head")
    x_place = (place // 2) % 2
    seq_total = CTX * ROWS

    none = jnp.zeros_like(query_up)
    ups = jnp.concatenate(
        [jnp.concatenate([query_up, none], 1), jnp.concatenate([none, value_up], 1)], 0
    )
    positions = (place * ROWS + jnp.arange(ROWS, dtype=jnp.int32)).astype(F32)
    freq = jnp.power(10000.0, -jnp.arange(64, dtype=F32) * 2.0 / HEAD_DIM)
    angle = positions[:, None] * freq[None, :]
    cosine, sine = jnp.cos(angle), jnp.sin(angle)
    table = jnp.stack(
        [jnp.concatenate([cosine, cosine], 1), jnp.concatenate([-sine, sine], 1)]
    )
    offsets = lax.dynamic_slice_in_dim(shifted, head_place * 2, 2) * 4
    spots = jnp.broadcast_to(jnp.mod(place - offsets, 8)[:, None], (2, 128)).astype(jnp.int32)

    (pack,) = whole([((4, 128, 256), BF)], pack_kernel, [w_query, w_key, w_value, w_out])
    other = swap_x(pack)
    parts = ring(pack, other, x_place)
    x_in, dy_in = whole([((ROWS, 512), BF)] * 2, order_kernel, [tokens, grad_out])
    x_in, dy_in, ups, table, spots = after((x_in, dy_in, ups, table, spots), other)
    x_parts = gather_head(x_in, head_place // 4)
    dy_parts = gather_head(after(dy_in, x_parts), head_place // 4)

    query, keyval, rinv, low, x8 = whole(
        [
            ((ROWS, 256), BF),
            ((2, ROWS, 256), BF),
            ((ROWS, 128), F32),
            ((ROWS, 16), BF),
            ((Z, ROWS, 512), BF),
        ],
        project_kernel,
        [query_down, value_down, ups, table, *x_parts],
        (parts, 0, 3),
        scratch=[pltpu.VMEM((Z, ROWS, 512), BF)],
        flops=2 * 256 * 4096 * 768,
    )
    own = [keyval] + [chips(keyval, step) for step in (1, 2, 3)]
    blocks = own + [swap_core(block) for block in own]
    d_context, down = whole(
        [((ROWS, 256), BF), ((4096, 48), BF)],
        context_grad_kernel,
        [query_down, value_down, *dy_parts],
        (parts, 3, 1),
        scratch=[pltpu.VMEM((Z, ROWS, 512), BF)],
        flops=2 * 256 * 4096 * 256,
    )
    partial, dq_pre, first, kept, sent = whole(
        [
            ((4, 2, ROWS, 512), BF),
            ((ROWS, 256), BF),
            ((2, ROWS, 256), F32),
            ((3, 2, ROWS, 256), BF),
            ((4, 2, ROWS, 256), BF),
        ],
        attention_kernel,
        [spots, query, d_context, table, *blocks],
        (parts, 3, 1),
        scratch=[
            pltpu.VMEM((8, ROWS, ROWS), F32),
            pltpu.VMEM((8, ROWS, ROWS), F32),
            pltpu.VMEM((ROWS, 256), BF),
        ],
        flops=24 * 256 * 2048 * 128,
    )
    chip_own, *chip_sums = whole(
        [((2, ROWS, 256), F32)] + [((2, ROWS, 256), BF)] * 3,
        combine_kernel,
        [first, kept, swap_core(sent)],
    )
    back = [chips(chip_sums[step - 1], step, True) for step in (1, 2, 3)]
    _, out_keep, out_got = sum_head(partial, chip_own)
    (output,) = whole([((ROWS, 512), BF)], output_kernel, [out_keep, out_got, tokens])
    pieces, grads, g3 = whole(
        [((CTX, 24, 128), F32), ((3, ROWS, 256), BF), ((ROWS, 48), BF)],
        small_kernel,
        [x8, rinv, low, ups, table, dq_pre, chip_own, *back],
        flops=2 * 256 * 4096 * 48,
    )
    (terms,) = whole(
        [((4, 2, ROWS + 16, 512), BF)],
        unproject_kernel,
        [x8, rinv, down, grads, g3],
        (parts, 0, 3),
        flops=2 * 256 * 4096 * 768,
    )
    got, keep, last = sum_head(terms)
    (grad_tokens,) = whole(
        [((ROWS, 512), BF)], finish_kernel, [tokens, grad_out, rinv, keep, last]
    )

    scale_out = 2.0 / seq_total**0.5
    first_sum = jnp.sum(lax.all_to_all(pieces, "ctx", 0, 0), axis=0) * scale_out
    second = jnp.sum(share(after(first_sum, got[0])[:16]), axis=0)
    third = after(jnp.concatenate([second, first_sum[16:]], 0), (output, keep))
    third = lax.all_to_all(jnp.broadcast_to(third[None], (CTX, 24, 128)), "ctx", 0, 0)
    down_q, down_v, up_q, up_v = whole(
        [((4096, 8), F32), ((4096, 8), F32), ((8, 256), F32), ((8, 256), F32)],
        spread_kernel,
        [third],
    )
    return (output, grad_tokens, down_q, up_q, down_v, up_v)


def solution(mesh):
    in_specs = (
        P("ctx", "head"),
        P("ctx", "head"),
        P("ctx", "head"),
        P("ctx", "head"),
        P("head", "ctx"),
        P(),
        P(None, "head"),
        P(),
        P(None, "head"),
        P(),
        P("ctx", "head"),
    )
    out_specs = (P("ctx", "head"), P("ctx", "head"), P(), P(None, "head"), P(), P(None, "head"))
    return jax.shard_map(
        per_device, mesh=mesh, in_specs=in_specs, out_specs=out_specs, check_vma=False
    )
```

```python
import jax
import jax.numpy as jnp
from jax import lax
from jax.experimental import pallas as pl
from jax.experimental.pallas import tpu as pltpu
from jax.sharding import PartitionSpec as P

HEAD_DIM = 128
BF = jnp.bfloat16
F32 = jnp.float32
CTX = 32
HEAD = 8
Z = 8
ROWS = 256
SCALE = 1.0 / HEAD_DIM**0.5
HIDDEN = -1e30
EARLY = 5
DELTA = (0, -1, 1, -2, 2, -3, 3, 4)
VMEM_LIMIT = 60 * 1024 * 1024


def move(value, axis, count, to):
    return lax.ppermute(value, axis, [(i, to(i)) for i in range(count)])


def swap_core(value):
    return move(value, "ctx", CTX, lambda i: i ^ 1)


def swap_x(value):
    return move(value, "ctx", CTX, lambda i: i ^ 2)


def along_z(value, step):
    return move(value, "ctx", CTX, lambda i: (i + 4 * step) % CTX)


def chips(value, step, back=False):
    pairs = [(i, (i + 2 * step) % CTX) for i in range(CTX)]
    if step == 3:
        pairs = [p for p in pairs if (p[1] // 2) % 2 == 1]
    if back:
        pairs = [(d, s) for s, d in pairs]
    return lax.ppermute(value, "ctx", pairs)


def ring(pack, other, x_place):
    block = jnp.where(
        x_place == 0,
        jnp.concatenate([pack, other], 1),
        jnp.concatenate([other, pack], 1),
    )
    up = down = block
    parts = [block]
    for _ in range(3):
        up = along_z(up, 1)
        down = along_z(down, -1)
        parts += [up, down]
    half = block.shape[1] // 2
    parts += [along_z(up[:, :half], 1), along_z(down[:, half:], -1)]
    return parts


def after(value, other):
    return lax.optimization_barrier((value, other))[0]


def nn(a, b):
    return jnp.dot(a, b, preferred_element_type=F32)


def nt(a, b):
    return lax.dot_general(a, b, (((1,), (1,)), ((), ())), preferred_element_type=F32)


def tn(a, b):
    return lax.dot_general(a, b, (((0,), (0,)), ((), ())), preferred_element_type=F32)


class Weights:
    def __init__(self, names, refs, buffers, sems, start, count):
        self.buffers = dict(zip(names, buffers))
        self.copies = {}
        for i, (name, ref, buffer) in enumerate(zip(names, refs, buffers)):
            copy = pltpu.make_async_copy(ref.at[pl.ds(start, count)], buffer, sems.at[i])
            copy.start()
            self.copies[name] = copy

    def one(self, name, j):
        if name in self.copies:
            self.copies.pop(name).wait()
        return self.buffers[name][j]

    def get(self, side, step, j):
        if step < 7:
            return self.one((side, step), j)
        return jnp.concatenate([self.one((side, 7), j), self.one((side, 8), j)], 0)


def whole(shape_dtypes, kernel, args, weights=None, leading=(), far=(), scratch=(), flops=0):
    args = list(args)
    specs = [pl.BlockSpec(memory_space=pltpu.VMEM)] * len(args)
    for array in leading:
        args.append(array)
        rank = array.ndim
        specs.append(
            pl.BlockSpec(
                (1,) + array.shape[1:],
                lambda i, rank=rank: (0,) * rank,
                pipeline_mode=pl.Buffered(1),
            )
        )
    for array in far:
        args.append(array)
        specs.append(pl.BlockSpec(memory_space=pl.ANY))
    scratch = list(scratch)
    plain = kernel
    if weights is not None:
        parts, start, count = weights
        names, arrays = list(parts), list(parts.values())
        n_in, n_w = len(args), len(arrays)
        args += arrays
        specs += [pl.BlockSpec(memory_space=pl.ANY)] * n_w
        scratch += [pltpu.VMEM((count,) + a.shape[1:], BF) for a in arrays]
        scratch += [pltpu.SemaphoreType.DMA((n_w,))]

        def plain(*refs):
            held = Weights(names, refs[n_in : n_in + n_w], refs[-n_w - 1 : -1], refs[-1], start, count)
            kernel(held, *refs[:n_in], *refs[n_in + n_w : -n_w - 1])

    moved = sum(a.size * a.dtype.itemsize for a in args)
    return pl.pallas_call(
        plain,
        grid=(1,),
        out_shape=[jax.ShapeDtypeStruct(s, d) for s, d in shape_dtypes],
        in_specs=specs,
        out_specs=[pl.BlockSpec(memory_space=pltpu.VMEM)] * len(shape_dtypes),
        scratch_shapes=scratch,
        compiler_params=pltpu.CompilerParams(vmem_limit_bytes=VMEM_LIMIT),
        cost_estimate=pl.CostEstimate(flops=flops, bytes_accessed=moved, transcendentals=0),
    )(*args)


def place_of():
    place = lax.axis_index("ctx")
    return place // 4, lax.rem(place, 2)


def head_of():
    place = lax.axis_index("head")
    return place // 4, lax.rem(place, 4)


def chunk_at(z, step):
    return lax.rem(z + (DELTA[step] + Z), Z)


def columns(core):
    return pl.ds(pl.multiple_of(core * 256, 256), 256)


def turn(v, table):
    return v * table[0] + pltpu.roll(v, 64, 1) * table[1]


def natural(v):
    return jnp.concatenate([v[:, :128], v[:, 256:384], v[:, 128:256], v[:, 384:]], 1)


def pack_kernel(w_query, w_key, w_value, w_out, pack):
    pack[0] = w_query[...]
    pack[1] = w_key[...]
    pack[2] = w_value[...]
    pack[3] = w_out[...].astype(F32).T.astype(BF)


def order_kernel(tokens, grad_out, x, dy):
    x[...] = natural(tokens[...])
    dy[...] = natural(grad_out[...])


def down_columns(array, i):
    return jnp.concatenate([array[:, i * 512 + a : i * 512 + a + 128] for a in (0, 256, 128, 384)], 1)


def chunk_of(k, x_low):
    return x_low * 4 + lax.rem(head_of()[1] + 4 - k, 4)


def sides():
    core = place_of()[1]
    return (0, core), (1, 1 - core)


def norm_kernel(down_q, down_v, *refs):
    got = refs[:4]
    normed, rinv_out, low_out, x_out = refs[4:]
    total = jnp.zeros((ROWS, 1), F32)
    for k in range(4):
        for x_low in range(2):
            raw = got[k][x_low]
            x_out[chunk_of(k, x_low)] = raw
            part = raw.astype(F32)
            total = total + jnp.sum(part * part, axis=1, keepdims=True)
    rinv = lax.rsqrt(total / 4096.0 + 1e-05)
    rinv_out[...] = jnp.broadcast_to(rinv, (ROWS, 128))
    low = jnp.zeros((ROWS, 16), F32)
    for i in range(Z):
        rounded = (x_out[i].astype(F32) * rinv).astype(BF)
        normed[i] = rounded
        pair = [down_columns(d, i).astype(F32) for d in (down_q, down_v)]
        low = low + nt(rounded, jnp.concatenate(pair, 0).astype(BF))
    low_out[...] = low.astype(BF)


def early_kernel(held, normed, acc_out):
    z = place_of()[0]
    acc = [jnp.zeros((ROWS, 256), F32) for _ in range(3)]
    for step in range(EARLY):
        here = chunk_at(z, step)
        for side, parity in sides():
            a = normed[here, :, columns(parity)]
            for j in range(3):
                acc[j] = acc[j] + nn(a, held.get(side, step, j))
    for j in range(3):
        acc_out[j] = acc[j]


def project_kernel(held, acc, low, ups, table, normed, query, keyval, chunks, sems):
    z = place_of()[0]
    copies = []
    for i in range(Z - EARLY):
        copy = pltpu.make_async_copy(normed.at[chunk_at(z, EARLY + i)], chunks.at[i], sems.at[i])
        copy.start()
        copies.append(copy)
    extra = 2.0 * nn(low[...], ups[...])
    lin = [acc[j] for j in range(3)]
    for i in range(Z - EARLY):
        copies[i].wait()
        for side, parity in sides():
            a = chunks[i, :, columns(parity)]
            for j in range(3):
                lin[j] = lin[j] + nn(a, held.get(side, EARLY + i, j))
    q_lin = lin[0] + extra[:, :256]
    for h in range(2):
        cols = slice(h * 128, h * 128 + 128)
        query[:, cols] = turn(q_lin[:, cols], table).astype(BF)
        keyval[0, :, cols] = turn(lin[1][:, cols], table).astype(BF)
    keyval[1] = (lin[2] + extra[:, 256:]).astype(BF)


def context_grad_kernel(held, down_q, down_v, *refs):
    got = refs[:4]
    out, down, dy = refs[4:]
    z = place_of()[0]
    for k in range(4):
        for x_low in range(2):
            dy[chunk_of(k, x_low)] = got[k][x_low]
    for i in range(Z):
        pair = [down_columns(d, i).astype(F32) for d in (down_q, down_v)]
        down[i] = jnp.concatenate(pair * 3, 0).astype(BF)
    acc = jnp.zeros((ROWS, 256), F32)
    for step in range(Z):
        here = chunk_at(z, step)
        for side, parity in sides():
            acc = acc + nn(dy[here, :, columns(parity)], held.get(side, step, 0))
    out[...] = acc.astype(BF)


def score_block(spots, q, key, b, head):
    core = place_of()[1]
    spot = spots[head : head + 1, :1]
    s = nt(q, key) * SCALE
    if b == 0:
        row = lax.broadcasted_iota(jnp.int32, (ROWS, ROWS), 0)
        col = lax.broadcasted_iota(jnp.int32, (ROWS, ROWS), 1)
        return jnp.where(col <= row, s, HIDDEN)
    behind = 2 * b if b < 4 else 2 * (b - 4) + 2 * core - 1
    if b == 4:
        return s + jnp.where(jnp.logical_and(spot >= behind, spot * 0 < behind), 0.0, HIDDEN)
    return s + jnp.where(spot >= behind, 0.0, HIDDEN)


def attention_kernel(held, spots, query, d_context, table, *refs):
    blocks = refs[:8]
    out, dq_out, first, kept, sent, probs, dprobs, context = refs[8:]
    z = place_of()[0]
    for head in range(2):
        cols = slice(head * 128, head * 128 + 128)
        q = query[:, cols]
        d_ctx = d_context[:, cols]
        top = jnp.full((ROWS, 1), HIDDEN, F32)
        for b in range(8):
            s = score_block(spots, q, blocks[b][0, :, cols], b, head)
            probs[b] = s
            top = jnp.maximum(top, jnp.max(s, axis=1, keepdims=True))
        total = jnp.zeros((ROWS, 1), F32)
        for b in range(8):
            e = jnp.exp(probs[b] - top)
            probs[b] = e
            total = total + jnp.sum(e, axis=1, keepdims=True)
        inv = 1.0 / total
        acc = jnp.zeros((ROWS, 128), F32)
        delta = jnp.zeros((ROWS, 1), F32)
        for b in range(8):
            prob = probs[b] * inv
            probs[b] = prob
            rounded = prob.astype(BF)
            value = blocks[b][1, :, cols]
            acc = acc + nn(rounded, value)
            dv = tn(rounded, d_ctx)
            dprob = nt(d_ctx, value)
            dprobs[b] = dprob
            delta = delta + jnp.sum(prob * dprob, axis=1, keepdims=True)
            if b == 0:
                first[1, :, cols] = dv
            elif b < 4:
                kept[b - 1, 1, :, cols] = dv.astype(BF)
            else:
                sent[b - 4, 1, :, cols] = dv.astype(BF)
        context[:, cols] = acc.astype(BF)
        dq = jnp.zeros((ROWS, 128), F32)
        for b in range(8):
            d_score = (probs[b] * (dprobs[b] - delta) * SCALE).astype(BF)
            dq = dq + nn(d_score, blocks[b][0, :, cols])
            dk = tn(d_score, q)
            if b == 0:
                first[0, :, cols] = dk
            elif b < 4:
                kept[b - 1, 0, :, cols] = dk.astype(BF)
            else:
                sent[b - 4, 0, :, cols] = dk.astype(BF)
        dq_out[:, cols] = (dq * table[0] - pltpu.roll(dq, 64, 1) * table[1]).astype(BF)
    y = head_of()[1]
    for step in range(Z):
        here = chunk_at(z, step)
        x_low, to = here // 4, lax.rem(lax.rem(here, 4) - y + 4, 4)
        for side, parity in sides():
            product = nt(context[...], held.get(side, step, 0))
            out[to, x_low, :, columns(parity)] = product.astype(BF)


def combine_kernel(first, kept, other, own, one, two, three):
    own[...] = first[...] + other[0].astype(F32)
    for t, out in enumerate((one, two, three)):
        out[...] = (kept[t].astype(F32) + other[t + 1].astype(F32)).astype(BF)


def along_y_kernel(one, two, three, mine, keep, send):
    x_low = head_of()[0]
    count = keep.shape[0]

    def total(at):
        parts = [mine[0, at], one[at], two[at], three[at]]
        result = parts[0].astype(F32)
        for part in parts[1:]:
            result = result + part.astype(F32)
        return result

    here, there = total(x_low), total(1 - x_low)
    keep[...] = here
    send[:ROWS] = there[:ROWS].astype(BF)
    if count > ROWS:
        sums = there[ROWS:, :ROWS] + there[ROWS:, ROWS:]
        high = sums.astype(BF)
        send[ROWS:, :ROWS] = high
        send[ROWS:, ROWS:] = (sums - high.astype(F32)).astype(BF)


def output_kernel(keep, got, tokens, out):
    total = keep[...] + got[...].astype(F32)
    out[...] = (tokens[...].astype(F32) + natural(total)).astype(BF)


def finish_kernel(tokens, grad_out, rinv, keep, got, out):
    total = keep[...] + got[...].astype(F32)
    sums = total[ROWS : ROWS + 8]
    sums = sums[:, :ROWS] + sums[:, ROWS:]
    row_mean = jnp.concatenate([sums] * 16, 0).T[:, :1] / 4096.0
    scale = rinv[:, :1]
    x_own = tokens[...].astype(F32) * scale
    out[...] = (
        grad_out[...].astype(F32) + scale * (natural(total[:ROWS]) - x_own * row_mean)
    ).astype(BF)


def spread_kernel(third, down_q, down_v, up_q, up_v):
    for c in range(CTX):
        down_q[:, c * 128 : c * 128 + 128] = third[c, :8]
        down_v[:, c * 128 : c * 128 + 128] = third[c, 8:16]
        out, row = (up_q, c // 2) if c < 16 else (up_v, c // 2 - 8)
        half = (c % 2) * 128
        out[row : row + 1, half : half + 128] = third[c, 16:17]


def small_kernel(x, rinv, low, ups, table, dq, own, one, two, three, out, grads, g_out):
    total = own[...] + one[...].astype(F32) + two[...].astype(F32) + three[...].astype(F32)
    grads[0] = dq[...]
    for h in range(2):
        cols = slice(h * 128, h * 128 + 128)
        v = total[0][:, cols]
        grads[1, :, cols] = (v * table[0] - pltpu.roll(v, 64, 1) * table[1]).astype(BF)
    grads[2] = total[1].astype(BF)
    pair = jnp.concatenate([grads[0], grads[2]], 1)
    g = nt(pair, ups[...])
    high = g.astype(BF)
    rest = g - high.astype(F32)
    middle = rest.astype(BF)
    low_part = (rest - middle.astype(F32)).astype(BF)
    g3 = jnp.concatenate([high, middle, low_part], 1)
    g_out[...] = g3
    scale = rinv[:, :1]
    for i in range(Z):
        normed = (x[i].astype(F32) * scale).astype(BF)
        r = tn(g3, normed)
        r = r[:16] + r[16:32] + r[32:48]
        for core in range(2):
            for x_place in range(2):
                at_col = (core * 2 + x_place) * 128
                out[i * 4 + x_place * 2 + core, :16, :] = r[:, at_col : at_col + 128]
    up = tn(low[...], pair)
    zero = jnp.zeros((7, 128), F32)
    for r in range(16):
        for half in range(2):
            col = half * 128 + (0 if r < 8 else 256)
            row = jnp.concatenate([up[r : r + 1, col : col + 128], zero], 0)
            out[2 * r + half, 16:24, :] = row


def unproject_kernel(held, x, rinv, down, grads, g3, out):
    z = place_of()[0]
    y = head_of()[1]
    scale = rinv[:, :1]
    rows = jnp.zeros((ROWS, 1), F32)
    for step in range(Z):
        here = chunk_at(z, step)
        x_low, to = here // 4, lax.rem(lax.rem(here, 4) - y + 4, 4)
        for side, parity in sides():
            cols = columns(parity)
            acc = 2.0 * nn(g3[...], down[here, :, cols])
            for j in range(3):
                acc = acc + nt(grads[j], held.get(side, step, j))
            xn = x[here, :, cols].astype(F32) * scale
            rows = rows + jnp.sum(acc * xn, axis=1, keepdims=True)
            out[to, x_low, :ROWS, cols] = acc.astype(BF)
    flat = jnp.broadcast_to(rows, (ROWS, 128)).T[:16]
    high = flat.astype(BF)
    rest = (flat - high.astype(F32)).astype(BF)
    for k in range(4):
        for x_low in range(2):
            out[k, x_low, ROWS:, :256] = high
            out[k, x_low, ROWS:, 256:] = rest


def swap_low(value):
    return move(value, "head", HEAD, lambda i: i ^ 4)


def along_y(value, step):
    return move(value, "head", HEAD, lambda i: (i // 4) * 4 + (i + step) % 4)


def gather_head(value, x_low):
    other = swap_low(value)
    both = jnp.where(x_low == 0, jnp.stack([value, other]), jnp.stack([other, value]))
    return [both] + [along_y(both, step) for step in (1, 2, 3)]


def sum_head(terms, hold=None):
    rows = terms.shape[2]
    sent = terms if hold is None else after(terms, hold)
    got = [along_y(sent[step], step) for step in (1, 2, 3)]
    keep, send = whole(
        [((rows, 512), F32), ((rows, 512), BF)], along_y_kernel, got, leading=[terms]
    )
    return got, keep, swap_low(send)


def per_device(
    tokens, w_query, w_key, w_value, w_out, query_down, query_up, value_down, value_up, shifted, grad_out
):
    place = lax.axis_index("ctx")
    head_place = lax.axis_index("head")
    x_place = (place // 2) % 2
    seq_total = CTX * ROWS

    none = jnp.zeros_like(query_up)
    ups = jnp.concatenate(
        [jnp.concatenate([query_up, none], 1), jnp.concatenate([none, value_up], 1)], 0
    )
    positions = (place * ROWS + jnp.arange(ROWS, dtype=jnp.int32)).astype(F32)
    freq = jnp.power(10000.0, -jnp.arange(64, dtype=F32) * 2.0 / HEAD_DIM)
    angle = positions[:, None] * freq[None, :]
    cosine, sine = jnp.cos(angle), jnp.sin(angle)
    table = jnp.stack(
        [jnp.concatenate([cosine, cosine], 1), jnp.concatenate([-sine, sine], 1)]
    )
    offsets = lax.dynamic_slice_in_dim(shifted, head_place * 2, 2) * 4
    spots = jnp.broadcast_to(jnp.mod(place - offsets, 8)[:, None], (2, 128)).astype(jnp.int32)

    (pack,) = whole([((4, 128, 256), BF)], pack_kernel, [w_query, w_key, w_value, w_out])
    other = swap_x(pack)
    x_in, dy_in = whole([((ROWS, 512), BF)] * 2, order_kernel, [tokens, grad_out])
    x_in, dy_in, ups, table, spots = after((x_in, dy_in, ups, table, spots), other)
    mine = ring(pack, other, x_place)
    x_parts = gather_head(x_in, head_place // 4)
    dy_parts = gather_head(after(dy_in, mine[7:]), head_place // 4)
    parts = {(0, i): part for i, part in enumerate(mine)}
    down_t = [query_down.T, value_down.T]

    normed, rinv, low, x8 = whole(
        [
            ((Z, ROWS, 512), BF),
            ((ROWS, 128), F32),
            ((ROWS, 16), BF),
            ((Z, ROWS, 512), BF),
        ],
        norm_kernel,
        [*down_t, *x_parts],
    )
    for i, part in enumerate(mine[:7]):
        parts[(1, i)] = swap_core(after(part, x_parts if i < 3 else normed))
    (acc,) = whole(
        [((3, ROWS, 256), F32)],
        early_kernel,
        [normed],
        ({name: part for name, part in parts.items() if name[1] < EARLY}, 0, 3),
        flops=2 * 256 * 512 * EARLY * 768,
    )
    for i, part in enumerate(mine[7:], 7):
        parts[(1, i)] = swap_core(after(part, acc))
    query, keyval = whole(
        [((ROWS, 256), BF), ((2, ROWS, 256), BF)],
        project_kernel,
        [acc, low, ups, table],
        ({name: part for name, part in parts.items() if name[1] >= EARLY}, 0, 3),
        far=[normed],
        scratch=[
            pltpu.VMEM((Z - EARLY, ROWS, 512), BF),
            pltpu.SemaphoreType.DMA((Z - EARLY,)),
        ],
        flops=2 * 256 * 512 * (Z - EARLY) * 768,
    )
    own = [keyval] + [chips(keyval, step) for step in (1, 2, 3)]
    blocks = own + [swap_core(block) for block in own]
    d_context, down = whole(
        [((ROWS, 256), BF), ((Z, 48, 512), BF)],
        context_grad_kernel,
        [*down_t, *dy_parts],
        (parts, 3, 1),
        scratch=[pltpu.VMEM((Z, ROWS, 512), BF)],
        flops=2 * 256 * 4096 * 256,
    )
    partial, dq_pre, first, kept, sent = whole(
        [
            ((4, 2, ROWS, 512), BF),
            ((ROWS, 256), BF),
            ((2, ROWS, 256), F32),
            ((3, 2, ROWS, 256), BF),
            ((4, 2, ROWS, 256), BF),
        ],
        attention_kernel,
        [spots, query, d_context, table, *blocks],
        (parts, 3, 1),
        scratch=[
            pltpu.VMEM((8, ROWS, ROWS), F32),
            pltpu.VMEM((8, ROWS, ROWS), F32),
            pltpu.VMEM((ROWS, 256), BF),
        ],
        flops=24 * 256 * 2048 * 128,
    )
    chip_own, *chip_sums = whole(
        [((2, ROWS, 256), F32)] + [((2, ROWS, 256), BF)] * 3,
        combine_kernel,
        [first, kept, swap_core(sent)],
    )
    back = [chips(chip_sums[step - 1], step, True) for step in (1, 2, 3)]
    out_parts, out_keep, out_got = sum_head(partial, chip_own)
    (output,) = whole([((ROWS, 512), BF)], output_kernel, [out_keep, out_got, tokens])
    pieces, grads, g3 = whole(
        [((CTX, 24, 128), F32), ((3, ROWS, 256), BF), ((ROWS, 48), BF)],
        small_kernel,
        [x8, rinv, low, ups, table, after(dq_pre, out_parts[:2]), chip_own, *back],
        flops=2 * 256 * 4096 * 48,
    )
    (terms,) = whole(
        [((4, 2, ROWS + 16, 512), BF)],
        unproject_kernel,
        [x8, rinv, down, after(grads, out_parts), g3],
        (parts, 0, 3),
        flops=2 * 256 * 4096 * 768,
    )
    first_sum = jnp.sum(after(lax.all_to_all(pieces, "ctx", 0, 0), terms), axis=0)
    got, keep, last = sum_head(terms, first_sum)
    (grad_tokens,) = whole(
        [((ROWS, 512), BF)], finish_kernel, [tokens, grad_out, rinv, keep, last]
    )

    scale_out = 2.0 / seq_total**0.5
    first_sum = first_sum * scale_out
    second = first_sum[:16]
    for step in (1, 2, 3):
        second = second + along_y(first_sum[:16], step)
    second = second + swap_low(second)
    third = jnp.concatenate([second, first_sum[16:]], 0)
    third = lax.all_to_all(jnp.broadcast_to(third[None], (CTX, 24, 128)), "ctx", 0, 0)
    down_q, down_v, up_q, up_v = whole(
        [((8, 4096), F32), ((8, 4096), F32), ((8, 256), F32), ((8, 256), F32)],
        spread_kernel,
        [third],
    )
    return (output, grad_tokens, down_q.T, up_q, down_v.T, up_v)


def solution(mesh):
    in_specs = (
        P("ctx", "head"),
        P("ctx", "head"),
        P("ctx", "head"),
        P("ctx", "head"),
        P("head", "ctx"),
        P(),
        P(None, "head"),
        P(),
        P(None, "head"),
        P(),
        P("ctx", "head"),
    )
    out_specs = (P("ctx", "head"), P("ctx", "head"), P(), P(None, "head"), P(), P(None, "head"))
    return jax.shard_map(
        per_device, mesh=mesh, in_specs=in_specs, out_specs=out_specs, check_vma=False
    )
```

```python
import jax
import jax.numpy as jnp
from jax import lax
from jax.experimental import pallas as pl
from jax.experimental.pallas import tpu as pltpu
from jax.sharding import PartitionSpec as P

HEAD_DIM = 128
BF = jnp.bfloat16
F32 = jnp.float32
CTX = 32
HEAD = 8
Z = 8
ROWS = 256
SCALE = 1.0 / HEAD_DIM**0.5
HIDDEN = -1e30
EARLY = 5
DELTA = (0, -1, 1, -2, 2, -3, 3, 4)
VMEM_LIMIT = 60 * 1024 * 1024


def move(value, axis, count, to):
    return lax.ppermute(value, axis, [(i, to(i)) for i in range(count)])


def swap_core(value):
    return move(value, "ctx", CTX, lambda i: i ^ 1)


def swap_x(value):
    return move(value, "ctx", CTX, lambda i: i ^ 2)


def along_z(value, step):
    return move(value, "ctx", CTX, lambda i: (i + 4 * step) % CTX)


def chips(value, step, back=False):
    pairs = [(i, (i + 2 * step) % CTX) for i in range(CTX)]
    if step == 3:
        pairs = [p for p in pairs if (p[1] // 2) % 2 == 1]
    if back:
        pairs = [(d, s) for s, d in pairs]
    return lax.ppermute(value, "ctx", pairs)


def ring(pack, other, x_place):
    block = jnp.where(
        x_place == 0,
        jnp.concatenate([pack, other], 1),
        jnp.concatenate([other, pack], 1),
    )
    up = down = block
    parts = [block]
    for _ in range(3):
        up = along_z(up, 1)
        down = along_z(down, -1)
        parts += [up, down]
    half = block.shape[1] // 2
    parts += [along_z(up[:, :half], 1), along_z(down[:, half:], -1)]
    return parts


def after(value, other):
    return lax.optimization_barrier((value, other))[0]


def nn(a, b):
    return jnp.dot(a, b, preferred_element_type=F32)


def nt(a, b):
    return lax.dot_general(a, b, (((1,), (1,)), ((), ())), preferred_element_type=F32)


def tn(a, b):
    return lax.dot_general(a, b, (((0,), (0,)), ((), ())), preferred_element_type=F32)


class Weights:
    def __init__(self, names, refs, buffers, sems, start, count, groups):
        self.buffers = dict(zip(names, buffers))
        self.groups = [[] for _ in groups]
        self.limits = groups
        for i, (name, ref, buffer) in enumerate(zip(names, refs, buffers)):
            copy = pltpu.make_async_copy(ref.at[pl.ds(start, count)], buffer, sems.at[i])
            copy.start()
            self.groups[self.group(name)].append(copy)

    def group(self, name):
        return min(i for i, limit in enumerate(self.limits) if name[1] < limit)

    def one(self, name, j):
        waiting = self.groups[self.group(name)]
        while waiting:
            waiting.pop(0).wait()
        return self.buffers[name][j]

    def get(self, side, step, j):
        if step < 7:
            return self.one((side, step), j)
        return jnp.concatenate([self.one((side, 7), j), self.one((side, 8), j)], 0)


def whole(shape_dtypes, kernel, args, weights=None, groups=(9,), leading=(), far=(), scratch=(), flops=0):
    args = list(args)
    specs = [pl.BlockSpec(memory_space=pltpu.VMEM)] * len(args)
    for array in leading:
        args.append(array)
        rank = array.ndim
        specs.append(
            pl.BlockSpec(
                (1,) + array.shape[1:],
                lambda i, rank=rank: (0,) * rank,
                pipeline_mode=pl.Buffered(1),
            )
        )
    for array in far:
        args.append(array)
        specs.append(pl.BlockSpec(memory_space=pl.ANY))
    scratch = list(scratch)
    plain = kernel
    if weights is not None:
        parts, start, count = weights
        names, arrays = list(parts), list(parts.values())
        n_in, n_w = len(args), len(arrays)
        args += arrays
        specs += [pl.BlockSpec(memory_space=pl.ANY)] * n_w
        scratch += [pltpu.VMEM((count,) + a.shape[1:], BF) for a in arrays]
        scratch += [pltpu.SemaphoreType.DMA((n_w,))]

        def plain(*refs):
            held = Weights(names, refs[n_in : n_in + n_w], refs[-n_w - 1 : -1], refs[-1], start, count, groups)
            kernel(held, *refs[:n_in], *refs[n_in + n_w : -n_w - 1])

    moved = sum(a.size * a.dtype.itemsize for a in args)
    return pl.pallas_call(
        plain,
        grid=(1,),
        out_shape=[jax.ShapeDtypeStruct(s, d) for s, d in shape_dtypes],
        in_specs=specs,
        out_specs=[pl.BlockSpec(memory_space=pltpu.VMEM)] * len(shape_dtypes),
        scratch_shapes=scratch,
        compiler_params=pltpu.CompilerParams(vmem_limit_bytes=VMEM_LIMIT),
        cost_estimate=pl.CostEstimate(flops=flops, bytes_accessed=moved, transcendentals=0),
    )(*args)


def place_of():
    place = lax.axis_index("ctx")
    return place // 4, lax.rem(place, 2)


def head_of():
    place = lax.axis_index("head")
    return place // 4, lax.rem(place, 4)


def chunk_at(z, step):
    return lax.rem(z + (DELTA[step] + Z), Z)


def columns(core):
    return pl.ds(pl.multiple_of(core * 256, 256), 256)


def turn(v, table):
    return v * table[0] + pltpu.roll(v, 64, 1) * table[1]


def natural(v):
    return jnp.concatenate([v[:, :128], v[:, 256:384], v[:, 128:256], v[:, 384:]], 1)


def pack_kernel(w_query, w_key, w_value, w_out, pack):
    pack[0] = w_query[...]
    pack[1] = w_key[...]
    pack[2] = w_value[...]
    pack[3] = w_out[...].astype(F32).T.astype(BF)


def order_kernel(tokens, grad_out, x, dy):
    x[...] = natural(tokens[...])
    dy[...] = natural(grad_out[...])


def down_columns(array, i):
    return jnp.concatenate([array[:, i * 512 + a : i * 512 + a + 128] for a in (0, 256, 128, 384)], 1)


def chunk_of(k, x_low):
    return x_low * 4 + lax.rem(head_of()[1] + 4 - k, 4)


def sides():
    core = place_of()[1]
    return (0, core), (1, 1 - core)


def norm_kernel(down_q, down_v, *refs):
    got = refs[:4]
    normed, rinv_out, low_out, x_out = refs[4:]
    total = jnp.zeros((ROWS, 1), F32)
    for k in range(4):
        for x_low in range(2):
            raw = got[k][x_low]
            x_out[chunk_of(k, x_low)] = raw
            part = raw.astype(F32)
            total = total + jnp.sum(part * part, axis=1, keepdims=True)
    rinv = lax.rsqrt(total / 4096.0 + 1e-05)
    rinv_out[...] = jnp.broadcast_to(rinv, (ROWS, 128))
    low = jnp.zeros((ROWS, 16), F32)
    for i in range(Z):
        rounded = (x_out[i].astype(F32) * rinv).astype(BF)
        normed[i] = rounded
        pair = [down_columns(d, i).astype(F32) for d in (down_q, down_v)]
        low = low + nt(rounded, jnp.concatenate(pair, 0).astype(BF))
    low_out[...] = low.astype(BF)


def early_kernel(held, normed, acc_out):
    z = place_of()[0]
    acc = [jnp.zeros((ROWS, 256), F32) for _ in range(3)]
    for step in range(EARLY):
        here = chunk_at(z, step)
        for side, parity in sides():
            a = normed[here, :, columns(parity)]
            for j in range(3):
                acc[j] = acc[j] + nn(a, held.get(side, step, j))
    for j in range(3):
        acc_out[j] = acc[j]


def project_kernel(held, acc, low, ups, table, normed, query, keyval, chunks, sems):
    z = place_of()[0]
    copies = []
    for i in range(Z - EARLY):
        copy = pltpu.make_async_copy(normed.at[chunk_at(z, EARLY + i)], chunks.at[i], sems.at[i])
        copy.start()
        copies.append(copy)
    extra = 2.0 * nn(low[...], ups[...])
    lin = [acc[j] for j in range(3)]
    for i in range(Z - EARLY):
        copies[i].wait()
        for side, parity in sides():
            a = chunks[i, :, columns(parity)]
            for j in range(3):
                lin[j] = lin[j] + nn(a, held.get(side, EARLY + i, j))
    q_lin = lin[0] + extra[:, :256]
    for h in range(2):
        cols = slice(h * 128, h * 128 + 128)
        query[:, cols] = turn(q_lin[:, cols], table).astype(BF)
        keyval[0, :, cols] = turn(lin[1][:, cols], table).astype(BF)
    keyval[1] = (lin[2] + extra[:, 256:]).astype(BF)


def context_grad_kernel(held, down_q, down_v, *refs):
    got = refs[:4]
    out, down, dy = refs[4:]
    z = place_of()[0]
    for k in range(4):
        for x_low in range(2):
            dy[chunk_of(k, x_low)] = got[k][x_low]
    for i in range(Z):
        pair = [down_columns(d, i).astype(F32) for d in (down_q, down_v)]
        down[i] = jnp.concatenate(pair * 3, 0).astype(BF)
    acc = jnp.zeros((ROWS, 256), F32)
    for step in range(Z):
        here = chunk_at(z, step)
        for side, parity in sides():
            acc = acc + nn(dy[here, :, columns(parity)], held.get(side, step, 0))
    out[...] = acc.astype(BF)


def score_block(spots, q, key, b, head):
    core = place_of()[1]
    spot = spots[head : head + 1, :1]
    s = nt(q, key) * SCALE
    if b == 0:
        row = lax.broadcasted_iota(jnp.int32, (ROWS, ROWS), 0)
        col = lax.broadcasted_iota(jnp.int32, (ROWS, ROWS), 1)
        return jnp.where(col <= row, s, HIDDEN)
    behind = 2 * b if b < 4 else 2 * (b - 4) + 2 * core - 1
    if b == 4:
        return s + jnp.where(jnp.logical_and(spot >= behind, spot * 0 < behind), 0.0, HIDDEN)
    return s + jnp.where(spot >= behind, 0.0, HIDDEN)


def attention_kernel(held, spots, query, d_context, table, *refs):
    blocks = refs[:8]
    out, dq_out, first, kept, sent, probs, dprobs, context = refs[8:]
    z = place_of()[0]
    for head in range(2):
        cols = slice(head * 128, head * 128 + 128)
        q = query[:, cols]
        d_ctx = d_context[:, cols]
        top = jnp.full((ROWS, 1), HIDDEN, F32)
        for b in range(8):
            s = score_block(spots, q, blocks[b][0, :, cols], b, head)
            probs[b] = s
            top = jnp.maximum(top, jnp.max(s, axis=1, keepdims=True))
        total = jnp.zeros((ROWS, 1), F32)
        for b in range(8):
            e = jnp.exp(probs[b] - top)
            probs[b] = e
            total = total + jnp.sum(e, axis=1, keepdims=True)
        inv = 1.0 / total
        acc = jnp.zeros((ROWS, 128), F32)
        delta = jnp.zeros((ROWS, 1), F32)
        for b in range(8):
            prob = probs[b] * inv
            probs[b] = prob
            rounded = prob.astype(BF)
            value = blocks[b][1, :, cols]
            acc = acc + nn(rounded, value)
            dv = tn(rounded, d_ctx)
            dprob = nt(d_ctx, value)
            dprobs[b] = dprob
            delta = delta + jnp.sum(prob * dprob, axis=1, keepdims=True)
            if b == 0:
                first[1, :, cols] = dv
            elif b < 4:
                kept[b - 1, 1, :, cols] = dv.astype(BF)
            else:
                sent[b - 4, 1, :, cols] = dv.astype(BF)
        context[:, cols] = acc.astype(BF)
        dq = jnp.zeros((ROWS, 128), F32)
        for b in range(8):
            d_score = (probs[b] * (dprobs[b] - delta) * SCALE).astype(BF)
            dq = dq + nn(d_score, blocks[b][0, :, cols])
            dk = tn(d_score, q)
            if b == 0:
                first[0, :, cols] = dk
            elif b < 4:
                kept[b - 1, 0, :, cols] = dk.astype(BF)
            else:
                sent[b - 4, 0, :, cols] = dk.astype(BF)
        dq_out[:, cols] = (dq * table[0] - pltpu.roll(dq, 64, 1) * table[1]).astype(BF)
    y = head_of()[1]
    for step in range(Z):
        here = chunk_at(z, step)
        x_low, to = here // 4, lax.rem(lax.rem(here, 4) - y + 4, 4)
        for side, parity in sides():
            product = nt(context[...], held.get(side, step, 0))
            out[to, x_low, :, columns(parity)] = product.astype(BF)


def combine_kernel(first, kept, other, own, one, two, three):
    own[...] = first[...] + other[0].astype(F32)
    for t, out in enumerate((one, two, three)):
        out[...] = (kept[t].astype(F32) + other[t + 1].astype(F32)).astype(BF)


def along_y_kernel(one, two, three, mine, keep, send):
    x_low = head_of()[0]
    count = keep.shape[0]

    def total(at):
        parts = [mine[0, at], one[at], two[at], three[at]]
        result = parts[0].astype(F32)
        for part in parts[1:]:
            result = result + part.astype(F32)
        return result

    here, there = total(x_low), total(1 - x_low)
    keep[...] = here
    send[:ROWS] = there[:ROWS].astype(BF)
    if count > ROWS:
        sums = there[ROWS:, :ROWS] + there[ROWS:, ROWS:]
        high = sums.astype(BF)
        send[ROWS:, :ROWS] = high
        send[ROWS:, ROWS:] = (sums - high.astype(F32)).astype(BF)


def output_kernel(keep, got, tokens, out):
    total = keep[...] + got[...].astype(F32)
    out[...] = (tokens[...].astype(F32) + natural(total)).astype(BF)


def finish_kernel(tokens, grad_out, rinv, keep, got, out):
    total = keep[...] + got[...].astype(F32)
    sums = total[ROWS : ROWS + 8]
    sums = sums[:, :ROWS] + sums[:, ROWS:]
    row_mean = jnp.concatenate([sums] * 16, 0).T[:, :1] / 4096.0
    scale = rinv[:, :1]
    x_own = tokens[...].astype(F32) * scale
    out[...] = (
        grad_out[...].astype(F32) + scale * (natural(total[:ROWS]) - x_own * row_mean)
    ).astype(BF)


def spread_kernel(third, down_q, down_v, up_q, up_v):
    for c in range(CTX):
        down_q[:, c * 128 : c * 128 + 128] = third[c, :8]
        down_v[:, c * 128 : c * 128 + 128] = third[c, 8:16]
        out, row = (up_q, c // 2) if c < 16 else (up_v, c // 2 - 8)
        half = (c % 2) * 128
        out[row : row + 1, half : half + 128] = third[c, 16:17]


def small_kernel(x, rinv, low, ups, table, dq, own, one, two, three, out, grads, g_out):
    total = own[...] + one[...].astype(F32) + two[...].astype(F32) + three[...].astype(F32)
    grads[0] = dq[...]
    for h in range(2):
        cols = slice(h * 128, h * 128 + 128)
        v = total[0][:, cols]
        grads[1, :, cols] = (v * table[0] - pltpu.roll(v, 64, 1) * table[1]).astype(BF)
    grads[2] = total[1].astype(BF)
    pair = jnp.concatenate([grads[0], grads[2]], 1)
    g = nt(pair, ups[...])
    high = g.astype(BF)
    rest = g - high.astype(F32)
    middle = rest.astype(BF)
    low_part = (rest - middle.astype(F32)).astype(BF)
    g3 = jnp.concatenate([high, middle, low_part], 1)
    g_out[...] = g3
    scale = rinv[:, :1]
    for i in range(Z):
        normed = (x[i].astype(F32) * scale).astype(BF)
        r = tn(g3, normed)
        r = r[:16] + r[16:32] + r[32:48]
        for core in range(2):
            for x_place in range(2):
                at_col = (core * 2 + x_place) * 128
                out[i * 4 + x_place * 2 + core, :16, :] = r[:, at_col : at_col + 128]
    up = tn(low[...], pair)
    zero = jnp.zeros((7, 128), F32)
    for r in range(16):
        for half in range(2):
            col = half * 128 + (0 if r < 8 else 256)
            row = jnp.concatenate([up[r : r + 1, col : col + 128], zero], 0)
            out[2 * r + half, 16:24, :] = row


def unproject_kernel(held, x, rinv, down, grads, g3, out):
    z = place_of()[0]
    y = head_of()[1]
    scale = rinv[:, :1]
    rows = jnp.zeros((ROWS, 1), F32)
    for step in range(Z):
        here = chunk_at(z, step)
        x_low, to = here // 4, lax.rem(lax.rem(here, 4) - y + 4, 4)
        for side, parity in sides():
            cols = columns(parity)
            acc = 2.0 * nn(g3[...], down[here, :, cols])
            for j in range(3):
                acc = acc + nt(grads[j], held.get(side, step, j))
            xn = x[here, :, cols].astype(F32) * scale
            rows = rows + jnp.sum(acc * xn, axis=1, keepdims=True)
            out[to, x_low, :ROWS, cols] = acc.astype(BF)
    flat = jnp.broadcast_to(rows, (ROWS, 128)).T[:16]
    high = flat.astype(BF)
    rest = (flat - high.astype(F32)).astype(BF)
    for k in range(4):
        for x_low in range(2):
            out[k, x_low, ROWS:, :256] = high
            out[k, x_low, ROWS:, 256:] = rest


def swap_low(value):
    return move(value, "head", HEAD, lambda i: i ^ 4)


def along_y(value, step):
    return move(value, "head", HEAD, lambda i: (i // 4) * 4 + (i + step) % 4)


def gather_head(value, x_low):
    other = swap_low(value)
    both = jnp.where(x_low == 0, jnp.stack([value, other]), jnp.stack([other, value]))
    return [both] + [along_y(both, step) for step in (1, 2, 3)]


def sum_head(terms, hold=None):
    rows = terms.shape[2]
    sent = terms if hold is None else after(terms, hold)
    got = [along_y(sent[step], step) for step in (1, 2, 3)]
    keep, send = whole(
        [((rows, 512), F32), ((rows, 512), BF)], along_y_kernel, got, leading=[terms]
    )
    return got, keep, swap_low(send)


def per_device(
    tokens, w_query, w_key, w_value, w_out, query_down, query_up, value_down, value_up, shifted, grad_out
):
    place = lax.axis_index("ctx")
    head_place = lax.axis_index("head")
    x_place = (place // 2) % 2
    seq_total = CTX * ROWS

    none = jnp.zeros_like(query_up)
    ups = jnp.concatenate(
        [jnp.concatenate([query_up, none], 1), jnp.concatenate([none, value_up], 1)], 0
    )
    positions = (place * ROWS + jnp.arange(ROWS, dtype=jnp.int32)).astype(F32)
    freq = jnp.power(10000.0, -jnp.arange(64, dtype=F32) * 2.0 / HEAD_DIM)
    angle = positions[:, None] * freq[None, :]
    cosine, sine = jnp.cos(angle), jnp.sin(angle)
    table = jnp.stack(
        [jnp.concatenate([cosine, cosine], 1), jnp.concatenate([-sine, sine], 1)]
    )
    offsets = lax.dynamic_slice_in_dim(shifted, head_place * 2, 2) * 4
    spots = jnp.broadcast_to(jnp.mod(place - offsets, 8)[:, None], (2, 128)).astype(jnp.int32)

    (pack,) = whole([((4, 128, 256), BF)], pack_kernel, [w_query, w_key, w_value, w_out])
    other = swap_x(pack)
    x_in, dy_in = whole([((ROWS, 512), BF)] * 2, order_kernel, [tokens, grad_out])
    x_in, dy_in, ups, table, spots = after((x_in, dy_in, ups, table, spots), other)
    mine = ring(pack, other, x_place)
    x_parts = gather_head(x_in, head_place // 4)
    dy_parts = gather_head(after(dy_in, mine[7:]), head_place // 4)
    parts = {(0, i): part for i, part in enumerate(mine)}
    down_t = [query_down.T, value_down.T]

    normed, rinv, low, x8 = whole(
        [
            ((Z, ROWS, 512), BF),
            ((ROWS, 128), F32),
            ((ROWS, 16), BF),
            ((Z, ROWS, 512), BF),
        ],
        norm_kernel,
        [*down_t, *x_parts],
    )
    for i, part in enumerate(mine[:7]):
        parts[(1, i)] = swap_core(after(part, x_parts if i < 3 else normed))
    (acc,) = whole(
        [((3, ROWS, 256), F32)],
        early_kernel,
        [normed],
        ({name: part for name, part in parts.items() if name[1] < EARLY}, 0, 3),
        flops=2 * 256 * 512 * EARLY * 768,
    )
    for i, part in enumerate(mine[7:], 7):
        parts[(1, i)] = swap_core(after(part, acc))
    query, keyval = whole(
        [((ROWS, 256), BF), ((2, ROWS, 256), BF)],
        project_kernel,
        [acc, low, ups, table],
        ({name: part for name, part in parts.items() if name[1] >= EARLY}, 0, 3),
        far=[normed],
        scratch=[
            pltpu.VMEM((Z - EARLY, ROWS, 512), BF),
            pltpu.SemaphoreType.DMA((Z - EARLY,)),
        ],
        flops=2 * 256 * 512 * (Z - EARLY) * 768,
    )
    own = [keyval] + [chips(keyval, step) for step in (1, 2, 3)]
    blocks = own + [swap_core(block) for block in own]
    d_context, down = whole(
        [((ROWS, 256), BF), ((Z, 48, 512), BF)],
        context_grad_kernel,
        [*down_t, *dy_parts],
        (parts, 3, 1),
        scratch=[pltpu.VMEM((Z, ROWS, 512), BF)],
        flops=2 * 256 * 4096 * 256,
    )
    partial, dq_pre, first, kept, sent = whole(
        [
            ((4, 2, ROWS, 512), BF),
            ((ROWS, 256), BF),
            ((2, ROWS, 256), F32),
            ((3, 2, ROWS, 256), BF),
            ((4, 2, ROWS, 256), BF),
        ],
        attention_kernel,
        [spots, query, d_context, table, *blocks],
        (parts, 3, 1),
        scratch=[
            pltpu.VMEM((8, ROWS, ROWS), F32),
            pltpu.VMEM((8, ROWS, ROWS), F32),
            pltpu.VMEM((ROWS, 256), BF),
        ],
        flops=24 * 256 * 2048 * 128,
    )
    chip_own, *chip_sums = whole(
        [((2, ROWS, 256), F32)] + [((2, ROWS, 256), BF)] * 3,
        combine_kernel,
        [first, kept, swap_core(sent)],
    )
    back = [chips(chip_sums[step - 1], step, True) for step in (1, 2, 3)]
    out_parts, out_keep, out_got = sum_head(partial, chip_own)
    (output,) = whole([((ROWS, 512), BF)], output_kernel, [out_keep, out_got, tokens])
    pieces, grads, g3 = whole(
        [((CTX, 24, 128), F32), ((3, ROWS, 256), BF), ((ROWS, 48), BF)],
        small_kernel,
        [x8, rinv, low, ups, table, dq_pre, chip_own, *back],
        flops=2 * 256 * 4096 * 48,
    )
    (terms,) = whole(
        [((4, 2, ROWS + 16, 512), BF)],
        unproject_kernel,
        [x8, rinv, down, grads, g3],
        (parts, 0, 3),
        groups=(2, 9),
        flops=2 * 256 * 4096 * 768,
    )
    first_sum = jnp.sum(lax.all_to_all(pieces, "ctx", 0, 0), axis=0)
    got, keep, last = sum_head(terms)
    (grad_tokens,) = whole(
        [((ROWS, 512), BF)], finish_kernel, [tokens, grad_out, rinv, keep, last]
    )

    scale_out = 2.0 / seq_total**0.5
    first_sum = after(first_sum, terms) * scale_out
    second = first_sum[:16]
    for step in (1, 2, 3):
        second = second + along_y(first_sum[:16], step)
    second = second + swap_low(second)
    third = after(jnp.concatenate([second, first_sum[16:]], 0), (output, got))
    third = lax.all_to_all(jnp.broadcast_to(third[None], (CTX, 24, 128)), "ctx", 0, 0)
    down_q, down_v, up_q, up_v = whole(
        [((8, 4096), F32), ((8, 4096), F32), ((8, 256), F32), ((8, 256), F32)],
        spread_kernel,
        [third],
    )
    return (output, grad_tokens, down_q.T, up_q, down_v.T, up_v)


def solution(mesh):
    in_specs = (
        P("ctx", "head"),
        P("ctx", "head"),
        P("ctx", "head"),
        P("ctx", "head"),
        P("head", "ctx"),
        P(),
        P(None, "head"),
        P(),
        P(None, "head"),
        P(),
        P("ctx", "head"),
    )
    out_specs = (P("ctx", "head"), P("ctx", "head"), P(), P(None, "head"), P(), P(None, "head"))
    return jax.shard_map(
        per_device, mesh=mesh, in_specs=in_specs, out_specs=out_specs, check_vma=False
    )
```

```python
import jax
import jax.numpy as jnp
from jax import lax
from jax.experimental import pallas as pl
from jax.experimental.pallas import tpu as pltpu
from jax.sharding import PartitionSpec as P

HEAD_DIM = 128
BF = jnp.bfloat16
F32 = jnp.float32
CTX = 32
HEAD = 8
Z = 8
ROWS = 256
SCALE = 1.0 / HEAD_DIM**0.5
HIDDEN = -1e30
EARLY = 5
DELTA = (0, -1, 1, -2, 2, -3, 3, 4)
VMEM_LIMIT = 60 * 1024 * 1024


def move(value, axis, count, to):
    return lax.ppermute(value, axis, [(i, to(i)) for i in range(count)])


def swap_core(value):
    return move(value, "ctx", CTX, lambda i: i ^ 1)


def swap_x(value):
    return move(value, "ctx", CTX, lambda i: i ^ 2)


def along_z(value, step):
    return move(value, "ctx", CTX, lambda i: (i + 4 * step) % CTX)


def chips(value, step, back=False):
    pairs = [(i, (i + 2 * step) % CTX) for i in range(CTX)]
    if step == 3:
        pairs = [p for p in pairs if (p[1] // 2) % 2 == 1]
    if back:
        pairs = [(d, s) for s, d in pairs]
    return lax.ppermute(value, "ctx", pairs)


def ring(pack, other, x_place):
    block = jnp.where(
        x_place == 0,
        jnp.concatenate([pack, other], 1),
        jnp.concatenate([other, pack], 1),
    )
    up = down = block
    parts = [block]
    for _ in range(3):
        up = along_z(up, 1)
        down = along_z(down, -1)
        parts += [up, down]
    half = block.shape[1] // 2
    parts += [along_z(up[:, :half], 1), along_z(down[:, half:], -1)]
    return parts


def after(value, other):
    return lax.optimization_barrier((value, other))[0]


def nn(a, b):
    return jnp.dot(a, b, preferred_element_type=F32)


def nt(a, b):
    return lax.dot_general(a, b, (((1,), (1,)), ((), ())), preferred_element_type=F32)


def tn(a, b):
    return lax.dot_general(a, b, (((0,), (0,)), ((), ())), preferred_element_type=F32)


class Weights:
    def __init__(self, names, refs, buffers, sems, start, count, groups):
        self.buffers = dict(zip(names, buffers))
        self.groups = [[] for _ in groups]
        self.limits = groups
        for i, (name, ref, buffer) in enumerate(zip(names, refs, buffers)):
            copy = pltpu.make_async_copy(ref.at[pl.ds(start, count)], buffer, sems.at[i])
            copy.start()
            self.groups[self.group(name)].append(copy)

    def group(self, name):
        return min(i for i, limit in enumerate(self.limits) if name[1] < limit)

    def one(self, name, j):
        waiting = self.groups[self.group(name)]
        while waiting:
            waiting.pop(0).wait()
        return self.buffers[name][j]

    def get(self, side, step, j):
        if step < 7:
            return self.one((side, step), j)
        return jnp.concatenate([self.one((side, 7), j), self.one((side, 8), j)], 0)


def whole(shape_dtypes, kernel, args, weights=None, groups=(9,), leading=(), far=(), scratch=(), flops=0):
    args = list(args)
    specs = [pl.BlockSpec(memory_space=pltpu.VMEM)] * len(args)
    for array in leading:
        args.append(array)
        rank = array.ndim
        specs.append(
            pl.BlockSpec(
                (1,) + array.shape[1:],
                lambda i, rank=rank: (0,) * rank,
                pipeline_mode=pl.Buffered(1),
            )
        )
    for array in far:
        args.append(array)
        specs.append(pl.BlockSpec(memory_space=pl.ANY))
    scratch = list(scratch)
    plain = kernel
    if weights is not None:
        parts, start, count = weights
        names, arrays = list(parts), list(parts.values())
        n_in, n_w = len(args), len(arrays)
        args += arrays
        specs += [pl.BlockSpec(memory_space=pl.ANY)] * n_w
        scratch += [pltpu.VMEM((count,) + a.shape[1:], BF) for a in arrays]
        scratch += [pltpu.SemaphoreType.DMA((n_w,))]

        def plain(*refs):
            held = Weights(names, refs[n_in : n_in + n_w], refs[-n_w - 1 : -1], refs[-1], start, count, groups)
            kernel(held, *refs[:n_in], *refs[n_in + n_w : -n_w - 1])

    moved = sum(a.size * a.dtype.itemsize for a in args)
    return pl.pallas_call(
        plain,
        grid=(1,),
        out_shape=[jax.ShapeDtypeStruct(s, d) for s, d in shape_dtypes],
        in_specs=specs,
        out_specs=[pl.BlockSpec(memory_space=pltpu.VMEM)] * len(shape_dtypes),
        scratch_shapes=scratch,
        compiler_params=pltpu.CompilerParams(vmem_limit_bytes=VMEM_LIMIT),
        cost_estimate=pl.CostEstimate(flops=flops, bytes_accessed=moved, transcendentals=0),
    )(*args)


def place_of():
    place = lax.axis_index("ctx")
    return place // 4, lax.rem(place, 2)


def head_of():
    place = lax.axis_index("head")
    return place // 4, lax.rem(place, 4)


def chunk_at(z, step):
    return lax.rem(z + (DELTA[step] + Z), Z)


def columns(core):
    return pl.ds(pl.multiple_of(core * 256, 256), 256)


def turn(v, table):
    return v * table[0] + pltpu.roll(v, 64, 1) * table[1]


def natural(v):
    return jnp.concatenate([v[:, :128], v[:, 256:384], v[:, 128:256], v[:, 384:]], 1)


def pack_kernel(w_query, w_key, w_value, w_out, pack):
    pack[0] = w_query[...]
    pack[1] = w_key[...]
    pack[2] = w_value[...]
    pack[3] = w_out[...].astype(F32).T.astype(BF)


def order_kernel(tokens, grad_out, x, dy):
    for k in range(HEAD):
        x[k] = natural(tokens[...])
        dy[k] = natural(grad_out[...])


def down_columns(array, i):
    return jnp.concatenate([array[:, i * 512 + a : i * 512 + a + 128] for a in (0, 256, 128, 384)], 1)


def sides():
    core = place_of()[1]
    return (0, core), (1, 1 - core)


def norm_kernel(down_q, down_v, x, normed, rinv_out, low_out):
    total = jnp.zeros((ROWS, 1), F32)
    for i in range(Z):
        part = x[i].astype(F32)
        total = total + jnp.sum(part * part, axis=1, keepdims=True)
    rinv = lax.rsqrt(total / 4096.0 + 1e-05)
    rinv_out[...] = jnp.broadcast_to(rinv, (ROWS, 128))
    low = jnp.zeros((ROWS, 16), F32)
    for i in range(Z):
        rounded = (x[i].astype(F32) * rinv).astype(BF)
        normed[i] = rounded
        pair = [down_columns(d, i).astype(F32) for d in (down_q, down_v)]
        low = low + nt(rounded, jnp.concatenate(pair, 0).astype(BF))
    low_out[...] = low.astype(BF)


def early_kernel(held, normed, acc_out):
    z = place_of()[0]
    acc = [jnp.zeros((ROWS, 256), F32) for _ in range(3)]
    for step in range(EARLY):
        here = chunk_at(z, step)
        for side, parity in sides():
            a = normed[here, :, columns(parity)]
            for j in range(3):
                acc[j] = acc[j] + nn(a, held.get(side, step, j))
    for j in range(3):
        acc_out[j] = acc[j]


def project_kernel(held, acc, low, ups, table, normed, query, keyval, chunks, sems):
    z = place_of()[0]
    copies = []
    for i in range(Z - EARLY):
        copy = pltpu.make_async_copy(normed.at[chunk_at(z, EARLY + i)], chunks.at[i], sems.at[i])
        copy.start()
        copies.append(copy)
    extra = 2.0 * nn(low[...], ups[...])
    lin = [acc[j] for j in range(3)]
    for i in range(Z - EARLY):
        copies[i].wait()
        for side, parity in sides():
            a = chunks[i, :, columns(parity)]
            for j in range(3):
                lin[j] = lin[j] + nn(a, held.get(side, EARLY + i, j))
    q_lin = lin[0] + extra[:, :256]
    for h in range(2):
        cols = slice(h * 128, h * 128 + 128)
        query[:, cols] = turn(q_lin[:, cols], table).astype(BF)
        keyval[0, :, cols] = turn(lin[1][:, cols], table).astype(BF)
    keyval[1] = (lin[2] + extra[:, 256:]).astype(BF)


def context_grad_kernel(held, down_q, down_v, dy, out, down):
    z = place_of()[0]
    for i in range(Z):
        pair = [down_columns(d, i).astype(F32) for d in (down_q, down_v)]
        down[i] = jnp.concatenate(pair * 3, 0).astype(BF)
    acc = jnp.zeros((ROWS, 256), F32)
    for step in range(Z):
        here = chunk_at(z, step)
        for side, parity in sides():
            acc = acc + nn(dy[here, :, columns(parity)], held.get(side, step, 0))
    out[...] = acc.astype(BF)


def score_block(spots, q, key, b, head):
    core = place_of()[1]
    spot = spots[head : head + 1, :1]
    s = nt(q, key) * SCALE
    if b == 0:
        row = lax.broadcasted_iota(jnp.int32, (ROWS, ROWS), 0)
        col = lax.broadcasted_iota(jnp.int32, (ROWS, ROWS), 1)
        return jnp.where(col <= row, s, HIDDEN)
    behind = 2 * b if b < 4 else 2 * (b - 4) + 2 * core - 1
    if b == 4:
        return s + jnp.where(jnp.logical_and(spot >= behind, spot * 0 < behind), 0.0, HIDDEN)
    return s + jnp.where(spot >= behind, 0.0, HIDDEN)


def attention_kernel(held, spots, query, d_context, table, *refs):
    blocks = refs[:8]
    out, dq_out, first, kept, sent, probs, dprobs, context = refs[8:]
    z = place_of()[0]
    for head in range(2):
        cols = slice(head * 128, head * 128 + 128)
        q = query[:, cols]
        d_ctx = d_context[:, cols]
        top = jnp.full((ROWS, 1), HIDDEN, F32)
        for b in range(8):
            s = score_block(spots, q, blocks[b][0, :, cols], b, head)
            probs[b] = s
            top = jnp.maximum(top, jnp.max(s, axis=1, keepdims=True))
        total = jnp.zeros((ROWS, 1), F32)
        for b in range(8):
            e = jnp.exp(probs[b] - top)
            probs[b] = e
            total = total + jnp.sum(e, axis=1, keepdims=True)
        inv = 1.0 / total
        acc = jnp.zeros((ROWS, 128), F32)
        delta = jnp.zeros((ROWS, 1), F32)
        for b in range(8):
            prob = probs[b] * inv
            probs[b] = prob
            rounded = prob.astype(BF)
            value = blocks[b][1, :, cols]
            acc = acc + nn(rounded, value)
            dv = tn(rounded, d_ctx)
            dprob = nt(d_ctx, value)
            dprobs[b] = dprob
            delta = delta + jnp.sum(prob * dprob, axis=1, keepdims=True)
            if b == 0:
                first[1, :, cols] = dv
            elif b < 4:
                kept[b - 1, 1, :, cols] = dv.astype(BF)
            else:
                sent[b - 4, 1, :, cols] = dv.astype(BF)
        context[:, cols] = acc.astype(BF)
        dq = jnp.zeros((ROWS, 128), F32)
        for b in range(8):
            d_score = (probs[b] * (dprobs[b] - delta) * SCALE).astype(BF)
            dq = dq + nn(d_score, blocks[b][0, :, cols])
            dk = tn(d_score, q)
            if b == 0:
                first[0, :, cols] = dk
            elif b < 4:
                kept[b - 1, 0, :, cols] = dk.astype(BF)
            else:
                sent[b - 4, 0, :, cols] = dk.astype(BF)
        dq_out[:, cols] = (dq * table[0] - pltpu.roll(dq, 64, 1) * table[1]).astype(BF)
    y = head_of()[1]
    for step in range(Z):
        here = chunk_at(z, step)
        x_low, to = here // 4, lax.rem(lax.rem(here, 4) - y + 4, 4)
        for side, parity in sides():
            product = nt(context[...], held.get(side, step, 0))
            out[to, x_low, :, columns(parity)] = product.astype(BF)


def combine_kernel(first, kept, other, own, one, two, three):
    own[...] = first[...] + other[0].astype(F32)
    for t, out in enumerate((one, two, three)):
        out[...] = (kept[t].astype(F32) + other[t + 1].astype(F32)).astype(BF)


def along_y_kernel(one, two, three, mine, keep, send):
    x_low = head_of()[0]
    count = keep.shape[0]

    def total(at):
        parts = [mine[0, at], one[at], two[at], three[at]]
        result = parts[0].astype(F32)
        for part in parts[1:]:
            result = result + part.astype(F32)
        return result

    here, there = total(x_low), total(1 - x_low)
    keep[...] = here
    send[:ROWS] = there[:ROWS].astype(BF)
    if count > ROWS:
        sums = there[ROWS:, :ROWS] + there[ROWS:, ROWS:]
        high = sums.astype(BF)
        send[ROWS:, :ROWS] = high
        send[ROWS:, ROWS:] = (sums - high.astype(F32)).astype(BF)


def output_kernel(keep, got, tokens, out):
    total = keep[...] + got[...].astype(F32)
    out[...] = (tokens[...].astype(F32) + natural(total)).astype(BF)


def finish_kernel(tokens, grad_out, rinv, keep, got, out):
    total = keep[...] + got[...].astype(F32)
    sums = total[ROWS : ROWS + 8]
    sums = sums[:, :ROWS] + sums[:, ROWS:]
    row_mean = jnp.concatenate([sums] * 16, 0).T[:, :1] / 4096.0
    scale = rinv[:, :1]
    x_own = tokens[...].astype(F32) * scale
    out[...] = (
        grad_out[...].astype(F32) + scale * (natural(total[:ROWS]) - x_own * row_mean)
    ).astype(BF)


def spread_kernel(third, down_q, down_v, up_q, up_v):
    for c in range(CTX):
        down_q[:, c * 128 : c * 128 + 128] = third[c, :8]
        down_v[:, c * 128 : c * 128 + 128] = third[c, 8:16]
        out, row = (up_q, c // 2) if c < 16 else (up_v, c // 2 - 8)
        half = (c % 2) * 128
        out[row : row + 1, half : half + 128] = third[c, 16:17]


def small_kernel(x, rinv, low, ups, table, dq, own, one, two, three, out, grads, g_out):
    total = own[...] + one[...].astype(F32) + two[...].astype(F32) + three[...].astype(F32)
    grads[0] = dq[...]
    for h in range(2):
        cols = slice(h * 128, h * 128 + 128)
        v = total[0][:, cols]
        grads[1, :, cols] = (v * table[0] - pltpu.roll(v, 64, 1) * table[1]).astype(BF)
    grads[2] = total[1].astype(BF)
    pair = jnp.concatenate([grads[0], grads[2]], 1)
    g = nt(pair, ups[...])
    high = g.astype(BF)
    rest = g - high.astype(F32)
    middle = rest.astype(BF)
    low_part = (rest - middle.astype(F32)).astype(BF)
    g3 = jnp.concatenate([high, middle, low_part], 1)
    g_out[...] = g3
    scale = rinv[:, :1]
    for i in range(Z):
        normed = (x[i].astype(F32) * scale).astype(BF)
        r = tn(g3, normed)
        r = r[:16] + r[16:32] + r[32:48]
        for core in range(2):
            for x_place in range(2):
                at_col = (core * 2 + x_place) * 128
                out[i * 4 + x_place * 2 + core, :16, :] = r[:, at_col : at_col + 128]
    up = tn(low[...], pair)
    zero = jnp.zeros((7, 128), F32)
    for r in range(16):
        for half in range(2):
            col = half * 128 + (0 if r < 8 else 256)
            row = jnp.concatenate([up[r : r + 1, col : col + 128], zero], 0)
            out[2 * r + half, 16:24, :] = row


def unproject_kernel(held, x, rinv, down, grads, g3, out):
    z = place_of()[0]
    y = head_of()[1]
    scale = rinv[:, :1]
    rows = jnp.zeros((ROWS, 1), F32)
    for step in range(Z):
        here = chunk_at(z, step)
        x_low, to = here // 4, lax.rem(lax.rem(here, 4) - y + 4, 4)
        for side, parity in sides():
            cols = columns(parity)
            acc = 2.0 * nn(g3[...], down[here, :, cols])
            for j in range(3):
                acc = acc + nt(grads[j], held.get(side, step, j))
            xn = x[here, :, cols].astype(F32) * scale
            rows = rows + jnp.sum(acc * xn, axis=1, keepdims=True)
            out[to, x_low, :ROWS, cols] = acc.astype(BF)
    flat = jnp.broadcast_to(rows, (ROWS, 128)).T[:16]
    high = flat.astype(BF)
    rest = (flat - high.astype(F32)).astype(BF)
    for k in range(4):
        for x_low in range(2):
            out[k, x_low, ROWS:, :256] = high
            out[k, x_low, ROWS:, 256:] = rest


def swap_low(value):
    return move(value, "head", HEAD, lambda i: i ^ 4)


def along_y(value, step):
    return move(value, "head", HEAD, lambda i: (i // 4) * 4 + (i + step) % 4)


def sum_head(terms, hold=None):
    rows = terms.shape[2]
    sent = terms if hold is None else after(terms, hold)
    got = [along_y(sent[step], step) for step in (1, 2, 3)]
    keep, send = whole(
        [((rows, 512), F32), ((rows, 512), BF)], along_y_kernel, got, leading=[terms]
    )
    return got, keep, swap_low(send)


def per_device(
    tokens, w_query, w_key, w_value, w_out, query_down, query_up, value_down, value_up, shifted, grad_out
):
    place = lax.axis_index("ctx")
    head_place = lax.axis_index("head")
    x_place = (place // 2) % 2
    seq_total = CTX * ROWS

    none = jnp.zeros_like(query_up)
    ups = jnp.concatenate(
        [jnp.concatenate([query_up, none], 1), jnp.concatenate([none, value_up], 1)], 0
    )
    positions = (place * ROWS + jnp.arange(ROWS, dtype=jnp.int32)).astype(F32)
    freq = jnp.power(10000.0, -jnp.arange(64, dtype=F32) * 2.0 / HEAD_DIM)
    angle = positions[:, None] * freq[None, :]
    cosine, sine = jnp.cos(angle), jnp.sin(angle)
    table = jnp.stack(
        [jnp.concatenate([cosine, cosine], 1), jnp.concatenate([-sine, sine], 1)]
    )
    offsets = lax.dynamic_slice_in_dim(shifted, head_place * 2, 2) * 4
    spots = jnp.broadcast_to(jnp.mod(place - offsets, 8)[:, None], (2, 128)).astype(jnp.int32)

    (pack,) = whole([((4, 128, 256), BF)], pack_kernel, [w_query, w_key, w_value, w_out])
    other = swap_x(pack)
    x_in, dy_in = whole([((HEAD, ROWS, 512), BF)] * 2, order_kernel, [tokens, grad_out])
    x_in, dy_in, ups, table, spots = after((x_in, dy_in, ups, table, spots), other)
    mine = ring(pack, other, x_place)
    x8 = lax.all_to_all(x_in, "head", 0, 0)
    dy8 = lax.all_to_all(after(dy_in, x8), "head", 0, 0)
    parts = {(0, i): part for i, part in enumerate(mine)}
    down_t = [query_down.T, value_down.T]

    normed, rinv, low = whole(
        [
            ((Z, ROWS, 512), BF),
            ((ROWS, 128), F32),
            ((ROWS, 16), BF),
        ],
        norm_kernel,
        [*down_t, x8],
    )
    for i, part in enumerate(mine[:7]):
        parts[(1, i)] = swap_core(after(part, normed) if i >= 3 else part)
    (acc,) = whole(
        [((3, ROWS, 256), F32)],
        early_kernel,
        [normed],
        ({name: part for name, part in parts.items() if name[1] < EARLY}, 0, 3),
        flops=2 * 256 * 512 * EARLY * 768,
    )
    for i, part in enumerate(mine[7:], 7):
        parts[(1, i)] = swap_core(after(part, acc))
    query, keyval = whole(
        [((ROWS, 256), BF), ((2, ROWS, 256), BF)],
        project_kernel,
        [acc, low, ups, table],
        ({name: part for name, part in parts.items() if name[1] >= EARLY}, 0, 3),
        far=[normed],
        scratch=[
            pltpu.VMEM((Z - EARLY, ROWS, 512), BF),
            pltpu.SemaphoreType.DMA((Z - EARLY,)),
        ],
        flops=2 * 256 * 512 * (Z - EARLY) * 768,
    )
    own = [keyval] + [chips(keyval, step) for step in (1, 2, 3)]
    blocks = own + [swap_core(block) for block in own]
    d_context, down = whole(
        [((ROWS, 256), BF), ((Z, 48, 512), BF)],
        context_grad_kernel,
        [*down_t, dy8],
        (parts, 3, 1),
        flops=2 * 256 * 4096 * 256,
    )
    partial, dq_pre, first, kept, sent = whole(
        [
            ((4, 2, ROWS, 512), BF),
            ((ROWS, 256), BF),
            ((2, ROWS, 256), F32),
            ((3, 2, ROWS, 256), BF),
            ((4, 2, ROWS, 256), BF),
        ],
        attention_kernel,
        [spots, query, d_context, table, *blocks],
        (parts, 3, 1),
        scratch=[
            pltpu.VMEM((8, ROWS, ROWS), F32),
            pltpu.VMEM((8, ROWS, ROWS), F32),
            pltpu.VMEM((ROWS, 256), BF),
        ],
        flops=24 * 256 * 2048 * 128,
    )
    chip_own, *chip_sums = whole(
        [((2, ROWS, 256), F32)] + [((2, ROWS, 256), BF)] * 3,
        combine_kernel,
        [first, kept, swap_core(sent)],
    )
    back = [chips(chip_sums[step - 1], step, True) for step in (1, 2, 3)]
    out_parts, out_keep, out_got = sum_head(partial, chip_own)
    (output,) = whole([((ROWS, 512), BF)], output_kernel, [out_keep, out_got, tokens])
    pieces, grads, g3 = whole(
        [((CTX, 24, 128), F32), ((3, ROWS, 256), BF), ((ROWS, 48), BF)],
        small_kernel,
        [x8, rinv, low, ups, table, dq_pre, chip_own, *back],
        flops=2 * 256 * 4096 * 48,
    )
    (terms,) = whole(
        [((4, 2, ROWS + 16, 512), BF)],
        unproject_kernel,
        [x8, rinv, down, grads, g3],
        (parts, 0, 3),
        groups=(2, 9),
        flops=2 * 256 * 4096 * 768,
    )
    got, keep, last = sum_head(terms)
    (grad_tokens,) = whole(
        [((ROWS, 512), BF)], finish_kernel, [tokens, grad_out, rinv, keep, last]
    )

    scale_out = 2.0 / seq_total**0.5
    first_sum = jnp.sum(lax.all_to_all(pieces, "ctx", 0, 0), axis=0) * scale_out
    sent = jnp.broadcast_to(after(first_sum, got[0])[None, :16], (HEAD, 16, 128))
    second = jnp.sum(lax.all_to_all(sent, "head", 0, 0), axis=0)
    third = after(jnp.concatenate([second, first_sum[16:]], 0), (output, keep))
    third = lax.all_to_all(jnp.broadcast_to(third[None], (CTX, 24, 128)), "ctx", 0, 0)
    down_q, down_v, up_q, up_v = whole(
        [((8, 4096), F32), ((8, 4096), F32), ((8, 256), F32), ((8, 256), F32)],
        spread_kernel,
        [third],
    )
    return (output, grad_tokens, down_q.T, up_q, down_v.T, up_v)


def solution(mesh):
    in_specs = (
        P("ctx", "head"),
        P("ctx", "head"),
        P("ctx", "head"),
        P("ctx", "head"),
        P("head", "ctx"),
        P(),
        P(None, "head"),
        P(),
        P(None, "head"),
        P(),
        P("ctx", "head"),
    )
    out_specs = (P("ctx", "head"), P("ctx", "head"), P(), P(None, "head"), P(), P(None, "head"))
    return jax.shard_map(
        per_device, mesh=mesh, in_specs=in_specs, out_specs=out_specs, check_vma=False
    )
```

```python
import jax
import jax.numpy as jnp
from jax import lax
from jax.experimental import pallas as pl
from jax.experimental.pallas import tpu as pltpu
from jax.sharding import PartitionSpec as P

HEAD_DIM = 128
BF = jnp.bfloat16
F32 = jnp.float32
CTX = 32
HEAD = 8
Z = 8
ROWS = 256
SCALE = 1.0 / HEAD_DIM**0.5
HIDDEN = -1e30
EARLY = 5
DELTA = (0, -1, 1, -2, 2, -3, 3, 4)
VMEM_LIMIT = 60 * 1024 * 1024


def move(value, axis, count, to):
    return lax.ppermute(value, axis, [(i, to(i)) for i in range(count)])


def swap_core(value):
    return move(value, "ctx", CTX, lambda i: i ^ 1)


def swap_x(value):
    return move(value, "ctx", CTX, lambda i: i ^ 2)


def along_z(value, step):
    return move(value, "ctx", CTX, lambda i: (i + 4 * step) % CTX)


def chips(value, step, back=False):
    pairs = [(i, (i + 2 * step) % CTX) for i in range(CTX)]
    if step == 3:
        pairs = [p for p in pairs if (p[1] // 2) % 2 == 1]
    if back:
        pairs = [(d, s) for s, d in pairs]
    return lax.ppermute(value, "ctx", pairs)


def ring(pack, other, x_place):
    block = jnp.where(
        x_place == 0,
        jnp.concatenate([pack, other], 1),
        jnp.concatenate([other, pack], 1),
    )
    up = down = block
    parts = [block]
    for _ in range(3):
        up = along_z(up, 1)
        down = along_z(down, -1)
        parts += [up, down]
    half = block.shape[1] // 2
    parts += [along_z(up[:, :half], 1), along_z(down[:, half:], -1)]
    return parts


def after(value, other):
    return lax.optimization_barrier((value, other))[0]


def nn(a, b):
    return jnp.dot(a, b, preferred_element_type=F32)


def nt(a, b):
    return lax.dot_general(a, b, (((1,), (1,)), ((), ())), preferred_element_type=F32)


def tn(a, b):
    return lax.dot_general(a, b, (((0,), (0,)), ((), ())), preferred_element_type=F32)


class Weights:
    def __init__(self, names, refs, buffers, sems, start, count, groups):
        self.buffers = dict(zip(names, buffers))
        self.groups = [[] for _ in groups]
        self.limits = groups
        for i, (name, ref, buffer) in enumerate(zip(names, refs, buffers)):
            copy = pltpu.make_async_copy(ref.at[pl.ds(start, count)], buffer, sems.at[i])
            copy.start()
            self.groups[self.group(name)].append(copy)

    def group(self, name):
        return min(i for i, limit in enumerate(self.limits) if name[1] < limit)

    def one(self, name, j):
        waiting = self.groups[self.group(name)]
        while waiting:
            waiting.pop(0).wait()
        return self.buffers[name][j]

    def get(self, side, step, j):
        if step < 7:
            return self.one((side, step), j)
        return jnp.concatenate([self.one((side, 7), j), self.one((side, 8), j)], 0)


def whole(shape_dtypes, kernel, args, weights=None, groups=(9,), leading=(), far=(), scratch=(), flops=0):
    args = list(args)
    specs = [pl.BlockSpec(memory_space=pltpu.VMEM)] * len(args)
    for array in leading:
        args.append(array)
        rank = array.ndim
        specs.append(
            pl.BlockSpec(
                (1,) + array.shape[1:],
                lambda i, rank=rank: (0,) * rank,
                pipeline_mode=pl.Buffered(1),
            )
        )
    for array in far:
        args.append(array)
        specs.append(pl.BlockSpec(memory_space=pl.ANY))
    scratch = list(scratch)
    plain = kernel
    if weights is not None:
        parts, start, count = weights
        names, arrays = list(parts), list(parts.values())
        n_in, n_w = len(args), len(arrays)
        args += arrays
        specs += [pl.BlockSpec(memory_space=pl.ANY)] * n_w
        scratch += [pltpu.VMEM((count,) + a.shape[1:], BF) for a in arrays]
        scratch += [pltpu.SemaphoreType.DMA((n_w,))]

        def plain(*refs):
            held = Weights(names, refs[n_in : n_in + n_w], refs[-n_w - 1 : -1], refs[-1], start, count, groups)
            kernel(held, *refs[:n_in], *refs[n_in + n_w : -n_w - 1])

    moved = sum(a.size * a.dtype.itemsize for a in args)
    return pl.pallas_call(
        plain,
        grid=(1,),
        out_shape=[jax.ShapeDtypeStruct(s, d) for s, d in shape_dtypes],
        in_specs=specs,
        out_specs=[pl.BlockSpec(memory_space=pltpu.VMEM)] * len(shape_dtypes),
        scratch_shapes=scratch,
        compiler_params=pltpu.CompilerParams(vmem_limit_bytes=VMEM_LIMIT),
        cost_estimate=pl.CostEstimate(flops=flops, bytes_accessed=moved, transcendentals=0),
    )(*args)


def place_of():
    place = lax.axis_index("ctx")
    return place // 4, lax.rem(place, 2)


def head_of():
    place = lax.axis_index("head")
    return place // 4, lax.rem(place, 4)


def chunk_at(z, step):
    return lax.rem(z + (DELTA[step] + Z), Z)


def columns(core):
    return pl.ds(pl.multiple_of(core * 256, 256), 256)


def turn(v, table):
    return v * table[0] + pltpu.roll(v, 64, 1) * table[1]


def natural(v):
    return jnp.concatenate([v[:, :128], v[:, 256:384], v[:, 128:256], v[:, 384:]], 1)


def pack_kernel(w_query, w_key, w_value, w_out, pack):
    pack[0] = w_query[...]
    pack[1] = w_key[...]
    pack[2] = w_value[...]
    pack[3] = w_out[...].astype(F32).T.astype(BF)


def order_kernel(tokens, grad_out, x, dy):
    for k in range(HEAD):
        x[k] = natural(tokens[...])
        dy[k] = natural(grad_out[...])


def down_columns(array, i):
    return jnp.concatenate([array[:, i * 512 + a : i * 512 + a + 128] for a in (0, 256, 128, 384)], 1)


def sides():
    core = place_of()[1]
    return (0, core), (1, 1 - core)


def norm_kernel(down_q, down_v, x, normed, rinv_out, low_out):
    total = jnp.zeros((ROWS, 1), F32)
    for i in range(Z):
        part = x[i].astype(F32)
        total = total + jnp.sum(part * part, axis=1, keepdims=True)
    rinv = lax.rsqrt(total / 4096.0 + 1e-05)
    rinv_out[...] = jnp.broadcast_to(rinv, (ROWS, 128))
    low = jnp.zeros((ROWS, 16), F32)
    for i in range(Z):
        rounded = (x[i].astype(F32) * rinv).astype(BF)
        normed[i] = rounded
        pair = [down_columns(d, i).astype(F32) for d in (down_q, down_v)]
        low = low + nt(rounded, jnp.concatenate(pair, 0).astype(BF))
    low_out[...] = low.astype(BF)


def early_kernel(held, normed, acc_out):
    z = place_of()[0]
    acc = [jnp.zeros((ROWS, 256), F32) for _ in range(3)]
    for step in range(EARLY):
        here = chunk_at(z, step)
        for side, parity in sides():
            a = normed[here, :, columns(parity)]
            for j in range(3):
                acc[j] = acc[j] + nn(a, held.get(side, step, j))
    for j in range(3):
        acc_out[j] = acc[j]


def project_kernel(held, acc, low, ups, table, normed, query, keyval, chunks, sems):
    z = place_of()[0]
    copies = []
    for i in range(Z - EARLY):
        copy = pltpu.make_async_copy(normed.at[chunk_at(z, EARLY + i)], chunks.at[i], sems.at[i])
        copy.start()
        copies.append(copy)
    extra = 2.0 * nn(low[...], ups[...])
    lin = [acc[j] for j in range(3)]
    for i in range(Z - EARLY):
        copies[i].wait()
        for side, parity in sides():
            a = chunks[i, :, columns(parity)]
            for j in range(3):
                lin[j] = lin[j] + nn(a, held.get(side, EARLY + i, j))
    q_lin = lin[0] + extra[:, :256]
    for h in range(2):
        cols = slice(h * 128, h * 128 + 128)
        query[:, cols] = turn(q_lin[:, cols], table).astype(BF)
        keyval[0, :, cols] = turn(lin[1][:, cols], table).astype(BF)
    keyval[1] = (lin[2] + extra[:, 256:]).astype(BF)


def context_grad_kernel(held, down_q, down_v, dy, out, down):
    z = place_of()[0]
    for i in range(Z):
        pair = [down_columns(d, i).astype(F32) for d in (down_q, down_v)]
        down[i] = jnp.concatenate(pair * 3, 0).astype(BF)
    acc = jnp.zeros((ROWS, 256), F32)
    for step in range(Z):
        here = chunk_at(z, step)
        for side, parity in sides():
            acc = acc + nn(dy[here, :, columns(parity)], held.get(side, step, 0))
    out[...] = acc.astype(BF)


def score_block(spots, q, key, b, head):
    core = place_of()[1]
    spot = spots[head : head + 1, :1]
    s = nt(q, key) * SCALE
    if b == 0:
        row = lax.broadcasted_iota(jnp.int32, (ROWS, ROWS), 0)
        col = lax.broadcasted_iota(jnp.int32, (ROWS, ROWS), 1)
        return jnp.where(col <= row, s, HIDDEN)
    behind = 2 * b if b < 4 else 2 * (b - 4) + 2 * core - 1
    if b == 4:
        return s + jnp.where(jnp.logical_and(spot >= behind, spot * 0 < behind), 0.0, HIDDEN)
    return s + jnp.where(spot >= behind, 0.0, HIDDEN)


def attention_kernel(held, spots, query, d_context, table, *refs):
    blocks = refs[:8]
    out, dq_out, first, kept, sent, probs, dprobs, context = refs[8:]
    z = place_of()[0]
    for head in range(2):
        cols = slice(head * 128, head * 128 + 128)
        q = query[:, cols]
        d_ctx = d_context[:, cols]
        top = jnp.full((ROWS, 1), HIDDEN, F32)
        for b in range(8):
            s = score_block(spots, q, blocks[b][0, :, cols], b, head)
            probs[b] = s
            top = jnp.maximum(top, jnp.max(s, axis=1, keepdims=True))
        total = jnp.zeros((ROWS, 1), F32)
        for b in range(8):
            e = jnp.exp(probs[b] - top)
            probs[b] = e
            total = total + jnp.sum(e, axis=1, keepdims=True)
        inv = 1.0 / total
        acc = jnp.zeros((ROWS, 128), F32)
        delta = jnp.zeros((ROWS, 1), F32)
        for b in range(8):
            prob = probs[b] * inv
            probs[b] = prob
            rounded = prob.astype(BF)
            value = blocks[b][1, :, cols]
            acc = acc + nn(rounded, value)
            dv = tn(rounded, d_ctx)
            dprob = nt(d_ctx, value)
            dprobs[b] = dprob
            delta = delta + jnp.sum(prob * dprob, axis=1, keepdims=True)
            if b == 0:
                first[1, :, cols] = dv
            elif b < 4:
                kept[b - 1, 1, :, cols] = dv.astype(BF)
            else:
                sent[b - 4, 1, :, cols] = dv.astype(BF)
        context[:, cols] = acc.astype(BF)
        dq = jnp.zeros((ROWS, 128), F32)
        for b in range(8):
            d_score = (probs[b] * (dprobs[b] - delta) * SCALE).astype(BF)
            dq = dq + nn(d_score, blocks[b][0, :, cols])
            dk = tn(d_score, q)
            if b == 0:
                first[0, :, cols] = dk
            elif b < 4:
                kept[b - 1, 0, :, cols] = dk.astype(BF)
            else:
                sent[b - 4, 0, :, cols] = dk.astype(BF)
        dq_out[:, cols] = (dq * table[0] - pltpu.roll(dq, 64, 1) * table[1]).astype(BF)
    y = head_of()[1]
    for step in range(Z):
        here = chunk_at(z, step)
        x_low, to = here // 4, lax.rem(lax.rem(here, 4) - y + 4, 4)
        for side, parity in sides():
            product = nt(context[...], held.get(side, step, 0))
            out[to, x_low, :, columns(parity)] = product.astype(BF)


def combine_kernel(first, kept, other, own, one, two, three):
    own[...] = first[...] + other[0].astype(F32)
    for t, out in enumerate((one, two, three)):
        out[...] = (kept[t].astype(F32) + other[t + 1].astype(F32)).astype(BF)


def along_y_kernel(one, two, three, mine, keep, send):
    x_low = head_of()[0]
    count = keep.shape[0]

    def total(at):
        parts = [mine[0, at], one[at], two[at], three[at]]
        result = parts[0].astype(F32)
        for part in parts[1:]:
            result = result + part.astype(F32)
        return result

    here, there = total(x_low), total(1 - x_low)
    keep[...] = here
    send[:ROWS] = there[:ROWS].astype(BF)
    if count > ROWS:
        sums = there[ROWS:, :ROWS] + there[ROWS:, ROWS:]
        high = sums.astype(BF)
        send[ROWS:, :ROWS] = high
        send[ROWS:, ROWS:] = (sums - high.astype(F32)).astype(BF)


def output_kernel(keep, got, tokens, out):
    total = keep[...] + got[...].astype(F32)
    out[...] = (tokens[...].astype(F32) + natural(total)).astype(BF)


def finish_kernel(tokens, grad_out, rinv, keep, got, out):
    total = keep[...] + got[...].astype(F32)
    sums = total[ROWS : ROWS + 8]
    sums = sums[:, :ROWS] + sums[:, ROWS:]
    row_mean = jnp.concatenate([sums] * 16, 0).T[:, :1] / 4096.0
    scale = rinv[:, :1]
    x_own = tokens[...].astype(F32) * scale
    out[...] = (
        grad_out[...].astype(F32) + scale * (natural(total[:ROWS]) - x_own * row_mean)
    ).astype(BF)


def spread_kernel(third, down_q, down_v, up_q, up_v):
    for c in range(CTX):
        down_q[:, c * 128 : c * 128 + 128] = third[c, :8]
        down_v[:, c * 128 : c * 128 + 128] = third[c, 8:16]
        out, row = (up_q, c // 2) if c < 16 else (up_v, c // 2 - 8)
        half = (c % 2) * 128
        out[row : row + 1, half : half + 128] = third[c, 16:17]


def small_kernel(x, rinv, low, ups, table, dq, own, one, two, three, out, grads, g_out):
    total = own[...] + one[...].astype(F32) + two[...].astype(F32) + three[...].astype(F32)
    grads[0] = dq[...]
    for h in range(2):
        cols = slice(h * 128, h * 128 + 128)
        v = total[0][:, cols]
        grads[1, :, cols] = (v * table[0] - pltpu.roll(v, 64, 1) * table[1]).astype(BF)
    grads[2] = total[1].astype(BF)
    pair = jnp.concatenate([grads[0], grads[2]], 1)
    g = nt(pair, ups[...])
    high = g.astype(BF)
    rest = g - high.astype(F32)
    middle = rest.astype(BF)
    low_part = (rest - middle.astype(F32)).astype(BF)
    g3 = jnp.concatenate([high, middle, low_part], 1)
    g_out[...] = g3
    scale = rinv[:, :1]
    for i in range(Z):
        normed = (x[i].astype(F32) * scale).astype(BF)
        r = tn(g3, normed)
        r = r[:16] + r[16:32] + r[32:48]
        for core in range(2):
            for x_place in range(2):
                at_col = (core * 2 + x_place) * 128
                out[i * 4 + x_place * 2 + core, :16, :] = r[:, at_col : at_col + 128]
    up = tn(low[...], pair)
    zero = jnp.zeros((7, 128), F32)
    for r in range(16):
        for half in range(2):
            col = half * 128 + (0 if r < 8 else 256)
            row = jnp.concatenate([up[r : r + 1, col : col + 128], zero], 0)
            out[2 * r + half, 16:24, :] = row


def unproject_kernel(held, x, rinv, down, grads, g3, out):
    z = place_of()[0]
    y = head_of()[1]
    scale = rinv[:, :1]
    rows = jnp.zeros((ROWS, 1), F32)
    for step in range(Z):
        here = chunk_at(z, step)
        x_low, to = here // 4, lax.rem(lax.rem(here, 4) - y + 4, 4)
        for side, parity in sides():
            cols = columns(parity)
            acc = 2.0 * nn(g3[...], down[here, :, cols])
            for j in range(3):
                acc = acc + nt(grads[j], held.get(side, step, j))
            xn = x[here, :, cols].astype(F32) * scale
            rows = rows + jnp.sum(acc * xn, axis=1, keepdims=True)
            out[to, x_low, :ROWS, cols] = acc.astype(BF)
    flat = jnp.broadcast_to(rows, (ROWS, 128)).T[:16]
    high = flat.astype(BF)
    rest = (flat - high.astype(F32)).astype(BF)
    for k in range(4):
        for x_low in range(2):
            out[k, x_low, ROWS:, :256] = high
            out[k, x_low, ROWS:, 256:] = rest


def swap_low(value):
    return move(value, "head", HEAD, lambda i: i ^ 4)


def along_y(value, step):
    return move(value, "head", HEAD, lambda i: (i // 4) * 4 + (i + step) % 4)


def sum_head(terms, hold=None):
    rows = terms.shape[2]
    sent = terms if hold is None else after(terms, hold)
    got = [along_y(sent[step], step) for step in (1, 2, 3)]
    keep, send = whole(
        [((rows, 512), F32), ((rows, 512), BF)], along_y_kernel, got, leading=[terms]
    )
    return got, keep, swap_low(send)


def per_device(
    tokens, w_query, w_key, w_value, w_out, query_down, query_up, value_down, value_up, shifted, grad_out
):
    place = lax.axis_index("ctx")
    head_place = lax.axis_index("head")
    x_place = (place // 2) % 2
    seq_total = CTX * ROWS

    none = jnp.zeros_like(query_up)
    ups = jnp.concatenate(
        [jnp.concatenate([query_up, none], 1), jnp.concatenate([none, value_up], 1)], 0
    )
    positions = (place * ROWS + jnp.arange(ROWS, dtype=jnp.int32)).astype(F32)
    freq = jnp.power(10000.0, -jnp.arange(64, dtype=F32) * 2.0 / HEAD_DIM)
    angle = positions[:, None] * freq[None, :]
    cosine, sine = jnp.cos(angle), jnp.sin(angle)
    table = jnp.stack(
        [jnp.concatenate([cosine, cosine], 1), jnp.concatenate([-sine, sine], 1)]
    )
    offsets = lax.dynamic_slice_in_dim(shifted, head_place * 2, 2) * 4
    spots = jnp.broadcast_to(jnp.mod(place - offsets, 8)[:, None], (2, 128)).astype(jnp.int32)

    (pack,) = whole([((4, 128, 256), BF)], pack_kernel, [w_query, w_key, w_value, w_out])
    other = swap_x(pack)
    x_in, dy_in = whole([((HEAD, ROWS, 512), BF)] * 2, order_kernel, [tokens, grad_out])
    x_in, dy_in, ups, table, spots = after((x_in, dy_in, ups, table, spots), other)
    mine = ring(pack, other, x_place)
    x8 = lax.all_to_all(x_in, "head", 0, 0)
    dy8 = lax.all_to_all(after(dy_in, x8), "head", 0, 0)
    parts = {(0, i): part for i, part in enumerate(mine)}
    down_t = [query_down.T, value_down.T]

    normed, rinv, low = whole(
        [
            ((Z, ROWS, 512), BF),
            ((ROWS, 128), F32),
            ((ROWS, 16), BF),
        ],
        norm_kernel,
        [*down_t, x8],
    )
    for i, part in enumerate(mine[:7]):
        parts[(1, i)] = swap_core(after(part, normed) if i >= 3 else part)
    (acc,) = whole(
        [((3, ROWS, 256), F32)],
        early_kernel,
        [normed],
        ({name: part for name, part in parts.items() if name[1] < EARLY}, 0, 3),
        flops=2 * 256 * 512 * EARLY * 768,
    )
    for i, part in enumerate(mine[7:], 7):
        parts[(1, i)] = swap_core(after(part, acc))
    query, keyval = whole(
        [((ROWS, 256), BF), ((2, ROWS, 256), BF)],
        project_kernel,
        [acc, low, ups, table],
        ({name: part for name, part in parts.items() if name[1] >= EARLY}, 0, 3),
        far=[normed],
        scratch=[
            pltpu.VMEM((Z - EARLY, ROWS, 512), BF),
            pltpu.SemaphoreType.DMA((Z - EARLY,)),
        ],
        flops=2 * 256 * 512 * (Z - EARLY) * 768,
    )
    own = [keyval] + [chips(keyval, step) for step in (1, 2, 3)]
    d_context, down = whole(
        [((ROWS, 256), BF), ((Z, 48, 512), BF)],
        context_grad_kernel,
        [*down_t, dy8],
        (parts, 3, 1),
        flops=2 * 256 * 4096 * 256,
    )
    blocks = own + [swap_core(keyval)] + [swap_core(after(b, d_context)) for b in own[1:]]
    partial, dq_pre, first, kept, sent = whole(
        [
            ((4, 2, ROWS, 512), BF),
            ((ROWS, 256), BF),
            ((2, ROWS, 256), F32),
            ((3, 2, ROWS, 256), BF),
            ((4, 2, ROWS, 256), BF),
        ],
        attention_kernel,
        [spots, query, d_context, table, *blocks],
        (parts, 3, 1),
        scratch=[
            pltpu.VMEM((8, ROWS, ROWS), F32),
            pltpu.VMEM((8, ROWS, ROWS), F32),
            pltpu.VMEM((ROWS, 256), BF),
        ],
        flops=24 * 256 * 2048 * 128,
    )
    chip_own, *chip_sums = whole(
        [((2, ROWS, 256), F32)] + [((2, ROWS, 256), BF)] * 3,
        combine_kernel,
        [first, kept, swap_core(sent)],
    )
    back = [chips(chip_sums[step - 1], step, True) for step in (1, 2, 3)]
    out_parts, out_keep, out_got = sum_head(partial, chip_own)
    (output,) = whole([((ROWS, 512), BF)], output_kernel, [out_keep, out_got, tokens])
    pieces, grads, g3 = whole(
        [((CTX, 24, 128), F32), ((3, ROWS, 256), BF), ((ROWS, 48), BF)],
        small_kernel,
        [x8, rinv, low, ups, table, dq_pre, chip_own, *back],
        flops=2 * 256 * 4096 * 48,
    )
    (terms,) = whole(
        [((4, 2, ROWS + 16, 512), BF)],
        unproject_kernel,
        [x8, rinv, down, grads, g3],
        (parts, 0, 3),
        groups=(2, 9),
        flops=2 * 256 * 4096 * 768,
    )
    got, keep, last = sum_head(terms)
    (grad_tokens,) = whole(
        [((ROWS, 512), BF)], finish_kernel, [tokens, grad_out, rinv, keep, last]
    )

    scale_out = 2.0 / seq_total**0.5
    first_sum = jnp.sum(lax.all_to_all(pieces, "ctx", 0, 0), axis=0) * scale_out
    sent = jnp.broadcast_to(after(first_sum, got[0])[None, :16], (HEAD, 16, 128))
    second = jnp.sum(lax.all_to_all(sent, "head", 0, 0), axis=0)
    third = after(jnp.concatenate([second, first_sum[16:]], 0), (output, got))
    third = lax.all_to_all(jnp.broadcast_to(third[None], (CTX, 24, 128)), "ctx", 0, 0)
    down_q, down_v, up_q, up_v = whole(
        [((8, 4096), F32), ((8, 4096), F32), ((8, 256), F32), ((8, 256), F32)],
        spread_kernel,
        [third],
    )
    return (output, grad_tokens, down_q.T, up_q, down_v.T, up_v)


def solution(mesh):
    in_specs = (
        P("ctx", "head"),
        P("ctx", "head"),
        P("ctx", "head"),
        P("ctx", "head"),
        P("head", "ctx"),
        P(),
        P(None, "head"),
        P(),
        P(None, "head"),
        P(),
        P("ctx", "head"),
    )
    out_specs = (P("ctx", "head"), P("ctx", "head"), P(), P(None, "head"), P(), P(None, "head"))
    return jax.shard_map(
        per_device, mesh=mesh, in_specs=in_specs, out_specs=out_specs, check_vma=False
    )
```

```python
import jax
import jax.numpy as jnp
from jax import lax
from jax.experimental import pallas as pl
from jax.experimental.pallas import tpu as pltpu
from jax.sharding import PartitionSpec as P

HEAD_DIM = 128
BF = jnp.bfloat16
F32 = jnp.float32
CTX = 32
HEAD = 8
Z = 8
ROWS = 256
SCALE = 1.0 / HEAD_DIM**0.5
HIDDEN = -1e30
EARLY = 5
DELTA = (0, -1, 1, -2, 2, -3, 3, 4)
VMEM_LIMIT = 60 * 1024 * 1024


def move(value, axis, count, to):
    return lax.ppermute(value, axis, [(i, to(i)) for i in range(count)])


def swap_core(value):
    return move(value, "ctx", CTX, lambda i: i ^ 1)


def swap_x(value):
    return move(value, "ctx", CTX, lambda i: i ^ 2)


def along_z(value, step):
    return move(value, "ctx", CTX, lambda i: (i + 4 * step) % CTX)


def chips(value, step, back=False):
    pairs = [(i, (i + 2 * step) % CTX) for i in range(CTX)]
    if step == 3:
        pairs = [p for p in pairs if (p[1] // 2) % 2 == 1]
    if back:
        pairs = [(d, s) for s, d in pairs]
    return lax.ppermute(value, "ctx", pairs)


def ring(pack, other, x_place):
    block = jnp.where(
        x_place == 0,
        jnp.concatenate([pack, other], 1),
        jnp.concatenate([other, pack], 1),
    )
    up = down = block
    parts = [block]
    for _ in range(3):
        up = along_z(up, 1)
        down = along_z(down, -1)
        parts += [up, down]
    half = block.shape[1] // 2
    parts += [along_z(up[:, :half], 1), along_z(down[:, half:], -1)]
    return parts


def after(value, other):
    return lax.optimization_barrier((value, other))[0]


def nn(a, b):
    return jnp.dot(a, b, preferred_element_type=F32)


def nt(a, b):
    return lax.dot_general(a, b, (((1,), (1,)), ((), ())), preferred_element_type=F32)


def tn(a, b):
    return lax.dot_general(a, b, (((0,), (0,)), ((), ())), preferred_element_type=F32)


class Weights:
    def __init__(self, names, refs, buffers, sems, start, count, groups):
        self.buffers = dict(zip(names, buffers))
        self.groups = [[] for _ in groups]
        self.limits = groups
        for i, (name, ref, buffer) in enumerate(zip(names, refs, buffers)):
            copy = pltpu.make_async_copy(ref.at[pl.ds(start, count)], buffer, sems.at[i])
            copy.start()
            self.groups[self.group(name)].append(copy)

    def group(self, name):
        return min(i for i, limit in enumerate(self.limits) if name[1] < limit)

    def one(self, name, j):
        waiting = self.groups[self.group(name)]
        while waiting:
            waiting.pop(0).wait()
        return self.buffers[name][j]

    def get(self, side, step, j):
        if step < 7:
            return self.one((side, step), j)
        return jnp.concatenate([self.one((side, 7), j), self.one((side, 8), j)], 0)


def whole(shape_dtypes, kernel, args, weights=None, groups=(9,), leading=(), far=(), scratch=(), flops=0):
    args = list(args)
    specs = [pl.BlockSpec(memory_space=pltpu.VMEM)] * len(args)
    for array in leading:
        args.append(array)
        rank = array.ndim
        specs.append(
            pl.BlockSpec(
                (1,) + array.shape[1:],
                lambda i, rank=rank: (0,) * rank,
                pipeline_mode=pl.Buffered(1),
            )
        )
    for array in far:
        args.append(array)
        specs.append(pl.BlockSpec(memory_space=pl.ANY))
    scratch = list(scratch)
    plain = kernel
    if weights is not None:
        parts, start, count = weights
        names, arrays = list(parts), list(parts.values())
        n_in, n_w = len(args), len(arrays)
        args += arrays
        specs += [pl.BlockSpec(memory_space=pl.ANY)] * n_w
        scratch += [pltpu.VMEM((count,) + a.shape[1:], BF) for a in arrays]
        scratch += [pltpu.SemaphoreType.DMA((n_w,))]

        def plain(*refs):
            held = Weights(names, refs[n_in : n_in + n_w], refs[-n_w - 1 : -1], refs[-1], start, count, groups)
            kernel(held, *refs[:n_in], *refs[n_in + n_w : -n_w - 1])

    moved = sum(a.size * a.dtype.itemsize for a in args)
    return pl.pallas_call(
        plain,
        grid=(1,),
        out_shape=[jax.ShapeDtypeStruct(s, d) for s, d in shape_dtypes],
        in_specs=specs,
        out_specs=[pl.BlockSpec(memory_space=pltpu.VMEM)] * len(shape_dtypes),
        scratch_shapes=scratch,
        compiler_params=pltpu.CompilerParams(vmem_limit_bytes=VMEM_LIMIT),
        cost_estimate=pl.CostEstimate(flops=flops, bytes_accessed=moved, transcendentals=0),
    )(*args)


def place_of():
    place = lax.axis_index("ctx")
    return place // 4, lax.rem(place, 2)


def head_of():
    place = lax.axis_index("head")
    return place // 4, lax.rem(place, 4)


def chunk_at(z, step):
    return lax.rem(z + (DELTA[step] + Z), Z)


def columns(core):
    return pl.ds(pl.multiple_of(core * 256, 256), 256)


def turn(v, table):
    return v * table[0] + pltpu.roll(v, 64, 1) * table[1]


def natural(v):
    return jnp.concatenate([v[:, :128], v[:, 256:384], v[:, 128:256], v[:, 384:]], 1)


def pack_kernel(w_query, w_key, w_value, w_out, pack):
    pack[0] = w_query[...]
    pack[1] = w_key[...]
    pack[2] = w_value[...]
    pack[3] = w_out[...].astype(F32).T.astype(BF)


def order_kernel(tokens, grad_out, x, dy):
    for k in range(HEAD):
        x[k] = natural(tokens[...])
        dy[k] = natural(grad_out[...])


def down_columns(array, i):
    return jnp.concatenate([array[:, i * 512 + a : i * 512 + a + 128] for a in (0, 256, 128, 384)], 1)


def sides():
    core = place_of()[1]
    return (0, core), (1, 1 - core)


def norm_kernel(down_q, down_v, x, normed, rinv_out, low_out):
    total = jnp.zeros((ROWS, 1), F32)
    for i in range(Z):
        part = x[i].astype(F32)
        total = total + jnp.sum(part * part, axis=1, keepdims=True)
    rinv = lax.rsqrt(total / 4096.0 + 1e-05)
    rinv_out[...] = jnp.broadcast_to(rinv, (ROWS, 128))
    low = jnp.zeros((ROWS, 16), F32)
    for i in range(Z):
        rounded = (x[i].astype(F32) * rinv).astype(BF)
        normed[i] = rounded
        pair = [down_columns(d, i).astype(F32) for d in (down_q, down_v)]
        low = low + nt(rounded, jnp.concatenate(pair, 0).astype(BF))
    low_out[...] = low.astype(BF)


def early_kernel(held, normed, acc_out):
    z = place_of()[0]
    acc = [jnp.zeros((ROWS, 256), F32) for _ in range(3)]
    for step in range(EARLY):
        here = chunk_at(z, step)
        for side, parity in sides():
            a = normed[here, :, columns(parity)]
            for j in range(3):
                acc[j] = acc[j] + nn(a, held.get(side, step, j))
    for j in range(3):
        acc_out[j] = acc[j]


def project_kernel(held, acc, low, ups, table, normed, query, keyval, chunks, sems):
    z = place_of()[0]
    copies = []
    for i in range(Z - EARLY):
        copy = pltpu.make_async_copy(normed.at[chunk_at(z, EARLY + i)], chunks.at[i], sems.at[i])
        copy.start()
        copies.append(copy)
    extra = 2.0 * nn(low[...], ups[...])
    lin = [acc[j] for j in range(3)]
    for i in range(Z - EARLY):
        copies[i].wait()
        for side, parity in sides():
            a = chunks[i, :, columns(parity)]
            for j in range(3):
                lin[j] = lin[j] + nn(a, held.get(side, EARLY + i, j))
    q_lin = lin[0] + extra[:, :256]
    for h in range(2):
        cols = slice(h * 128, h * 128 + 128)
        query[:, cols] = turn(q_lin[:, cols], table).astype(BF)
        keyval[0, :, cols] = turn(lin[1][:, cols], table).astype(BF)
    keyval[1] = (lin[2] + extra[:, 256:]).astype(BF)


def context_grad_kernel(held, down_q, down_v, dy, out, down):
    z = place_of()[0]
    for i in range(Z):
        pair = [down_columns(d, i).astype(F32) for d in (down_q, down_v)]
        down[i] = jnp.concatenate(pair * 3, 0).astype(BF)
    acc = jnp.zeros((ROWS, 256), F32)
    for step in range(Z):
        here = chunk_at(z, step)
        for side, parity in sides():
            acc = acc + nn(dy[here, :, columns(parity)], held.get(side, step, 0))
    out[...] = acc.astype(BF)


def score_block(spots, q, key, b, head):
    core = place_of()[1]
    spot = spots[head : head + 1, :1]
    s = nt(q, key) * SCALE
    if b == 0:
        row = lax.broadcasted_iota(jnp.int32, (ROWS, ROWS), 0)
        col = lax.broadcasted_iota(jnp.int32, (ROWS, ROWS), 1)
        return jnp.where(col <= row, s, HIDDEN)
    behind = 2 * b if b < 4 else 2 * (b - 4) + 2 * core - 1
    if b == 4:
        return s + jnp.where(jnp.logical_and(spot >= behind, spot * 0 < behind), 0.0, HIDDEN)
    return s + jnp.where(spot >= behind, 0.0, HIDDEN)


def attention_kernel(held, spots, query, d_context, table, *refs):
    blocks = refs[:8]
    out, dq_out, first, kept, sent, probs, dprobs, context = refs[8:]
    z = place_of()[0]
    for head in range(2):
        cols = slice(head * 128, head * 128 + 128)
        q = query[:, cols]
        d_ctx = d_context[:, cols]
        top = jnp.full((ROWS, 1), HIDDEN, F32)
        for b in range(8):
            s = score_block(spots, q, blocks[b][0, :, cols], b, head)
            probs[b] = s
            top = jnp.maximum(top, jnp.max(s, axis=1, keepdims=True))
        total = jnp.zeros((ROWS, 1), F32)
        for b in range(8):
            e = jnp.exp(probs[b] - top)
            probs[b] = e
            total = total + jnp.sum(e, axis=1, keepdims=True)
        inv = 1.0 / total
        acc = jnp.zeros((ROWS, 128), F32)
        delta = jnp.zeros((ROWS, 1), F32)
        for b in range(8):
            prob = probs[b] * inv
            probs[b] = prob
            rounded = prob.astype(BF)
            value = blocks[b][1, :, cols]
            acc = acc + nn(rounded, value)
            dv = tn(rounded, d_ctx)
            dprob = nt(d_ctx, value)
            dprobs[b] = dprob
            delta = delta + jnp.sum(prob * dprob, axis=1, keepdims=True)
            if b == 0:
                first[1, :, cols] = dv
            elif b < 4:
                kept[b - 1, 1, :, cols] = dv.astype(BF)
            else:
                sent[b - 4, 1, :, cols] = dv.astype(BF)
        context[:, cols] = acc.astype(BF)
        dq = jnp.zeros((ROWS, 128), F32)
        for b in range(8):
            d_score = (probs[b] * (dprobs[b] - delta) * SCALE).astype(BF)
            dq = dq + nn(d_score, blocks[b][0, :, cols])
            dk = tn(d_score, q)
            if b == 0:
                first[0, :, cols] = dk
            elif b < 4:
                kept[b - 1, 0, :, cols] = dk.astype(BF)
            else:
                sent[b - 4, 0, :, cols] = dk.astype(BF)
        dq_out[:, cols] = (dq * table[0] - pltpu.roll(dq, 64, 1) * table[1]).astype(BF)
    y = head_of()[1]
    for step in range(Z):
        here = chunk_at(z, step)
        x_low, to = here // 4, lax.rem(lax.rem(here, 4) - y + 4, 4)
        for side, parity in sides():
            product = nt(context[...], held.get(side, step, 0))
            out[to, x_low, :, columns(parity)] = product.astype(BF)


def combine_kernel(first, kept, other, own, one, two, three):
    own[...] = first[...] + other[0].astype(F32)
    for t, out in enumerate((one, two, three)):
        out[...] = (kept[t].astype(F32) + other[t + 1].astype(F32)).astype(BF)


def along_y_kernel(one, two, three, mine, keep, send):
    x_low = head_of()[0]
    count = keep.shape[0]

    def total(at):
        parts = [mine[0, at], one[at], two[at], three[at]]
        result = parts[0].astype(F32)
        for part in parts[1:]:
            result = result + part.astype(F32)
        return result

    here, there = total(x_low), total(1 - x_low)
    keep[...] = here
    send[:ROWS] = there[:ROWS].astype(BF)
    if count > ROWS:
        sums = there[ROWS:, :ROWS] + there[ROWS:, ROWS:]
        high = sums.astype(BF)
        send[ROWS:, :ROWS] = high
        send[ROWS:, ROWS:] = (sums - high.astype(F32)).astype(BF)


def output_kernel(keep, one, two, tokens, out):
    total = keep[...] + jnp.concatenate([one[...], two[...]], 0).astype(F32)
    out[...] = (tokens[...].astype(F32) + natural(total)).astype(BF)


def finish_kernel(tokens, grad_out, rinv, keep, one, two, out):
    total = keep[...] + jnp.concatenate([one[...], two[...]], 0).astype(F32)
    sums = total[ROWS : ROWS + 8]
    sums = sums[:, :ROWS] + sums[:, ROWS:]
    row_mean = jnp.concatenate([sums] * 16, 0).T[:, :1] / 4096.0
    scale = rinv[:, :1]
    x_own = tokens[...].astype(F32) * scale
    out[...] = (
        grad_out[...].astype(F32) + scale * (natural(total[:ROWS]) - x_own * row_mean)
    ).astype(BF)


def spread_kernel(third, down_q, down_v, up_q, up_v):
    for c in range(CTX):
        down_q[:, c * 128 : c * 128 + 128] = third[c, :8]
        down_v[:, c * 128 : c * 128 + 128] = third[c, 8:16]
        out, row = (up_q, c // 2) if c < 16 else (up_v, c // 2 - 8)
        half = (c % 2) * 128
        out[row : row + 1, half : half + 128] = third[c, 16:17]


def small_kernel(x, rinv, low, ups, table, dq, own, one, two, three, out, grads, g_out):
    total = own[...] + one[...].astype(F32) + two[...].astype(F32) + three[...].astype(F32)
    grads[0] = dq[...]
    for h in range(2):
        cols = slice(h * 128, h * 128 + 128)
        v = total[0][:, cols]
        grads[1, :, cols] = (v * table[0] - pltpu.roll(v, 64, 1) * table[1]).astype(BF)
    grads[2] = total[1].astype(BF)
    pair = jnp.concatenate([grads[0], grads[2]], 1)
    g = nt(pair, ups[...])
    high = g.astype(BF)
    rest = g - high.astype(F32)
    middle = rest.astype(BF)
    low_part = (rest - middle.astype(F32)).astype(BF)
    g3 = jnp.concatenate([high, middle, low_part], 1)
    g_out[...] = g3
    scale = rinv[:, :1]
    for i in range(Z):
        normed = (x[i].astype(F32) * scale).astype(BF)
        r = tn(g3, normed)
        r = r[:16] + r[16:32] + r[32:48]
        for core in range(2):
            for x_place in range(2):
                at_col = (core * 2 + x_place) * 128
                out[i * 4 + x_place * 2 + core, :16, :] = r[:, at_col : at_col + 128]
    up = tn(low[...], pair)
    zero = jnp.zeros((7, 128), F32)
    for r in range(16):
        for half in range(2):
            col = half * 128 + (0 if r < 8 else 256)
            row = jnp.concatenate([up[r : r + 1, col : col + 128], zero], 0)
            out[2 * r + half, 16:24, :] = row


def unproject_kernel(held, x, rinv, down, grads, g3, out):
    z = place_of()[0]
    y = head_of()[1]
    scale = rinv[:, :1]
    rows = jnp.zeros((ROWS, 1), F32)
    for step in range(Z):
        here = chunk_at(z, step)
        x_low, to = here // 4, lax.rem(lax.rem(here, 4) - y + 4, 4)
        for side, parity in sides():
            cols = columns(parity)
            acc = 2.0 * nn(g3[...], down[here, :, cols])
            for j in range(3):
                acc = acc + nt(grads[j], held.get(side, step, j))
            xn = x[here, :, cols].astype(F32) * scale
            rows = rows + jnp.sum(acc * xn, axis=1, keepdims=True)
            out[to, x_low, :ROWS, cols] = acc.astype(BF)
    flat = jnp.broadcast_to(rows, (ROWS, 128)).T[:16]
    high = flat.astype(BF)
    rest = (flat - high.astype(F32)).astype(BF)
    for k in range(4):
        for x_low in range(2):
            out[k, x_low, ROWS:, :256] = high
            out[k, x_low, ROWS:, 256:] = rest


def swap_low(value):
    return move(value, "head", HEAD, lambda i: i ^ 4)


def along_y(value, step):
    return move(value, "head", HEAD, lambda i: (i // 4) * 4 + (i + step) % 4)


def sum_head(terms, hold=None):
    rows = terms.shape[2]
    sent = terms if hold is None else after(terms, hold)
    got = [along_y(sent[step], step) for step in (1, 2, 3)]
    keep, send = whole(
        [((rows, 512), F32), ((rows, 512), BF)], along_y_kernel, got, leading=[terms]
    )
    half = rows // 32 * 16
    return got, keep, [swap_low(send[:half]), swap_low(send[half:])]


def per_device(
    tokens, w_query, w_key, w_value, w_out, query_down, query_up, value_down, value_up, shifted, grad_out
):
    place = lax.axis_index("ctx")
    head_place = lax.axis_index("head")
    x_place = (place // 2) % 2
    seq_total = CTX * ROWS

    none = jnp.zeros_like(query_up)
    ups = jnp.concatenate(
        [jnp.concatenate([query_up, none], 1), jnp.concatenate([none, value_up], 1)], 0
    )
    positions = (place * ROWS + jnp.arange(ROWS, dtype=jnp.int32)).astype(F32)
    freq = jnp.power(10000.0, -jnp.arange(64, dtype=F32) * 2.0 / HEAD_DIM)
    angle = positions[:, None] * freq[None, :]
    cosine, sine = jnp.cos(angle), jnp.sin(angle)
    table = jnp.stack(
        [jnp.concatenate([cosine, cosine], 1), jnp.concatenate([-sine, sine], 1)]
    )
    offsets = lax.dynamic_slice_in_dim(shifted, head_place * 2, 2) * 4
    spots = jnp.broadcast_to(jnp.mod(place - offsets, 8)[:, None], (2, 128)).astype(jnp.int32)

    (pack,) = whole([((4, 128, 256), BF)], pack_kernel, [w_query, w_key, w_value, w_out])
    other = swap_x(pack)
    x_in, dy_in = whole([((HEAD, ROWS, 512), BF)] * 2, order_kernel, [tokens, grad_out])
    x_in, dy_in, ups, table, spots = after((x_in, dy_in, ups, table, spots), other)
    mine = ring(pack, other, x_place)
    x8 = lax.all_to_all(x_in, "head", 0, 0)
    dy8 = lax.all_to_all(after(dy_in, x8), "head", 0, 0)
    parts = {(0, i): part for i, part in enumerate(mine)}
    down_t = [query_down.T, value_down.T]

    normed, rinv, low = whole(
        [
            ((Z, ROWS, 512), BF),
            ((ROWS, 128), F32),
            ((ROWS, 16), BF),
        ],
        norm_kernel,
        [*down_t, x8],
    )
    for i, part in enumerate(mine[:7]):
        parts[(1, i)] = swap_core(after(part, normed) if i >= 3 else part)
    (acc,) = whole(
        [((3, ROWS, 256), F32)],
        early_kernel,
        [normed],
        ({name: part for name, part in parts.items() if name[1] < EARLY}, 0, 3),
        flops=2 * 256 * 512 * EARLY * 768,
    )
    for i, part in enumerate(mine[7:], 7):
        parts[(1, i)] = swap_core(after(part, acc))
    query, keyval = whole(
        [((ROWS, 256), BF), ((2, ROWS, 256), BF)],
        project_kernel,
        [acc, low, ups, table],
        ({name: part for name, part in parts.items() if name[1] >= EARLY}, 0, 3),
        far=[normed],
        scratch=[
            pltpu.VMEM((Z - EARLY, ROWS, 512), BF),
            pltpu.SemaphoreType.DMA((Z - EARLY,)),
        ],
        flops=2 * 256 * 512 * (Z - EARLY) * 768,
    )
    own = [keyval] + [chips(keyval, step) for step in (1, 2, 3)]
    d_context, down = whole(
        [((ROWS, 256), BF), ((Z, 48, 512), BF)],
        context_grad_kernel,
        [*down_t, dy8],
        (parts, 3, 1),
        flops=2 * 256 * 4096 * 256,
    )
    blocks = own + [swap_core(keyval)] + [swap_core(after(b, d_context)) for b in own[1:]]
    partial, dq_pre, first, kept, sent = whole(
        [
            ((4, 2, ROWS, 512), BF),
            ((ROWS, 256), BF),
            ((2, ROWS, 256), F32),
            ((3, 2, ROWS, 256), BF),
            ((4, 2, ROWS, 256), BF),
        ],
        attention_kernel,
        [spots, query, d_context, table, *blocks],
        (parts, 3, 1),
        scratch=[
            pltpu.VMEM((8, ROWS, ROWS), F32),
            pltpu.VMEM((8, ROWS, ROWS), F32),
            pltpu.VMEM((ROWS, 256), BF),
        ],
        flops=24 * 256 * 2048 * 128,
    )
    chip_own, *chip_sums = whole(
        [((2, ROWS, 256), F32)] + [((2, ROWS, 256), BF)] * 3,
        combine_kernel,
        [first, kept, swap_core(sent)],
    )
    back = [chips(chip_sums[step - 1], step, True) for step in (1, 2, 3)]
    out_parts, out_keep, out_got = sum_head(partial, chip_own)
    (output,) = whole([((ROWS, 512), BF)], output_kernel, [out_keep, *out_got, tokens])
    pieces, grads, g3 = whole(
        [((CTX, 24, 128), F32), ((3, ROWS, 256), BF), ((ROWS, 48), BF)],
        small_kernel,
        [x8, rinv, low, ups, table, dq_pre, chip_own, *back],
        flops=2 * 256 * 4096 * 48,
    )
    (terms,) = whole(
        [((4, 2, ROWS + 16, 512), BF)],
        unproject_kernel,
        [x8, rinv, down, grads, g3],
        (parts, 0, 3),
        groups=(2, 9),
        flops=2 * 256 * 4096 * 768,
    )
    got, keep, last = sum_head(terms)
    (grad_tokens,) = whole(
        [((ROWS, 512), BF)], finish_kernel, [tokens, grad_out, rinv, keep, *last]
    )

    scale_out = 2.0 / seq_total**0.5
    first_sum = jnp.sum(lax.all_to_all(pieces, "ctx", 0, 0), axis=0) * scale_out
    sent = jnp.broadcast_to(after(first_sum, got[0])[None, :16], (HEAD, 16, 128))
    second = jnp.sum(lax.all_to_all(sent, "head", 0, 0), axis=0)
    third = after(jnp.concatenate([second, first_sum[16:]], 0), (output, last[0]))
    third = lax.all_to_all(jnp.broadcast_to(third[None], (CTX, 24, 128)), "ctx", 0, 0)
    down_q, down_v, up_q, up_v = whole(
        [((8, 4096), F32), ((8, 4096), F32), ((8, 256), F32), ((8, 256), F32)],
        spread_kernel,
        [third],
    )
    return (output, grad_tokens, down_q.T, up_q, down_v.T, up_v)


def solution(mesh):
    in_specs = (
        P("ctx", "head"),
        P("ctx", "head"),
        P("ctx", "head"),
        P("ctx", "head"),
        P("head", "ctx"),
        P(),
        P(None, "head"),
        P(),
        P(None, "head"),
        P(),
        P("ctx", "head"),
    )
    out_specs = (P("ctx", "head"), P("ctx", "head"), P(), P(None, "head"), P(), P(None, "head"))
    return jax.shard_map(
        per_device, mesh=mesh, in_specs=in_specs, out_specs=out_specs, check_vma=False
    )
```
